1024 devices in a mesh: dp: 16 (over z), expert: 64 (over x, y, core).
Axes of the slice: x: 4, y: 8, z: 16, core: 2. Of those that a mesh axis runs over, the one named last changes fastest.
Arguments:
- acts: bfloat16 [1024, 4096], P('expert', 'dp'), may hold values from -6 to 6
- grad_out: bfloat16 [1024, 4096], P('expert', 'dp'), may hold values from -18 to 18
- routes: int32 [1024, 8], P('expert'), may hold values from 0 to 63, all different within a row; in each aligned block of 16 rows (0 to 15, 16 to 31, ...) at most 3 rows name the same one
- combine: float32 [1024, 8], P('expert'), may hold values from 0.05 to 0.4
- w_gate: bfloat16 [64, 4096, 768], P('expert', 'dp'), may hold values from -0.09375 to 0.09375
- w_up: bfloat16 [64, 4096, 768], P('expert', 'dp'), may hold values from -0.09375 to 0.09375
- w_down: bfloat16 [64, 768, 4096], P('expert', None, 'dp'), may hold values from -0.21875 to 0.21875
Outputs:
- grad_acts: bfloat16 [1024, 4096], P('expert', 'dp')
- grad_gate_w: bfloat16 [64, 4096, 768], P('expert', 'dp')
- grad_up_w: bfloat16 [64, 4096, 768], P('expert', 'dp')
- grad_down_w: bfloat16 [64, 768, 4096], P('expert', None, 'dp')
The draws below stay inside these ranges and needn't reach their ends.
Inputs may be any that keep to these rules, and one draw needn't show every extreme that they name: `routes`: each row names 8 different experts. Among the rows of one index of the expert axis (aligned blocks of 16 tokens), no expert is named by more than 3 rows, a bound that some block reaches.
All inputs are finite; a program needn't handle non-finite values.
Results may differ from the reference program's by a relative error of at most 0.0064.
Values may be sent and summed in bfloat16 or wider, within the bound.
No kernel may reach another device: no remote copies, remote signals or barrier semaphores. Data moves between devices by JAX's collectives and lax.ppermute only.
A program may use at most 32 MiB of HBM per device.

```python
import math
import jax
import jax.numpy as jnp
import numpy as np
from jax import lax

D = 4096
FF = 768
TOP = 8
TOK_DEV = 16
EXPERTS = 64
TOKENS = 1024
CAP = 3
ROWS = 192


def level_of(own_key, shape, pieces, low, top_value):
    loudness, own = 1.0, jax.random.fold_in(own_key, 6)
    for position, blocks in pieces:
        steps = jnp.exp(jax.random.uniform(jax.random.fold_in(own, position), (blocks,), jnp.float32, low / len(pieces), top_value / len(pieces)))
        loudness = loudness * jnp.repeat(steps, shape[position] // blocks).reshape([-1 if axis == position else 1 for axis in range(len(shape))])
    return loudness


def shared_out(stream_key, own, number, rows, amount, top, limit, slope):
    sequence = jax.random.permutation(stream_key, amount)
    crowded, common = portions_of(amount, rows * top, limit, slope, True), portions_of(amount, rows * top, limit, slope, False)
    places = jnp.arange(amount)

    def named(sizes, offset_by):
        used = int((sizes > 0).sum())
        fixed = max(1, used // 4)
        moved = fixed + (places - fixed + offset_by * (used - fixed)) % max(1, amount - fixed)
        return jnp.zeros((amount,), jnp.int32).at[sequence[jnp.where(places < fixed, places, moved)]].set(jnp.asarray(sizes, jnp.int32))

    sizes = jnp.where(number % 4 == 0, named(crowded, number // 4), named(common, number - number // 4 - 1))
    mixed = jax.random.permutation(jax.random.fold_in(own, 3), amount)
    donor, receiver = mixed[0:amount // 2 * 2:2], mixed[1:amount // 2 * 2:2]
    slack = jnp.minimum(sizes[donor] - 1, limit - sizes[receiver]) // 2
    slack = jnp.where((donor == sequence[0]) | (receiver == sequence[0]) | (sizes[receiver] == 0), 0, jnp.maximum(slack, 0))
    moved = jax.random.randint(jax.random.fold_in(own, 4), (amount // 2,), 0, 1 << 20) % (slack + 1)
    sizes = sizes.at[donor].add(-moved).at[receiver].add(moved)
    items = jnp.searchsorted(jnp.cumsum(sizes), jnp.arange(rows * top), side="right").astype(jnp.int32)
    listing = items.reshape(top, rows).T
    listing = listing[jax.random.permutation(jax.random.fold_in(own, 1), rows)]
    offset_by = jax.random.randint(jax.random.fold_in(own, 2), (rows, 1), 0, top)
    return jnp.take_along_axis(listing, (jnp.arange(top)[None, :] + offset_by) % top, axis=1)


def portions_of(count, total, bound, skew, full):
    portions = [(1 << 20) // math.isqrt(standing ** skew) + 1 for standing in range(1, count + 1)]
    largest = bound if full else min(bound, max(-(-total // count), total * portions[0] // sum(portions)))
    least = 1 if total - largest >= count - 1 else 0
    counts, surplus = [largest] + [least] * (count - 1), total - largest - least * (count - 1)
    while surplus > 0:
        free = [i for i in range(1, count) if counts[i] < largest] or [i for i in range(1, count) if counts[i] < bound]
        whole, remaining = sum([portions[i] for i in free]), surplus
        for i in free:
            addition = min(bound - counts[i], max(1, remaining * portions[i] // whole), surplus)
            counts[i] = counts[i] + addition
            surplus = surplus - addition
    return np.array(counts)


def scatter_about(own_key, shape, spread, most, shards=(), held_as=jnp.bfloat16):
    entries = spread * jax.random.normal(own_key, shape, jnp.float32)
    if shards:
        entries = entries * level_of(own_key, shape, shards, -0.22, 0.18)
    return jnp.clip(entries, -most, most).astype(held_as)


def setup_inputs(seed: int = 0) -> dict:
    key_list = jax.random.split(jax.random.key(seed), 8)
    acts = scatter_about(key_list[0], (TOKENS, D), 1.0, 6.0, ((0, 64), (1, 16)))
    grad_out = scatter_about(key_list[1], (TOKENS, D), 3.0, 18.0, ((0, 64), (1, 16)))
    routes_keys = jax.random.split(jax.random.fold_in(key_list[2], 1), TOKENS // TOK_DEV)
    routes_turns = jax.random.permutation(jax.random.fold_in(key_list[2], 3), TOKENS // TOK_DEV)
    routes = jax.vmap(lambda own, number: shared_out(jax.random.fold_in(key_list[2], 2), own, number, TOK_DEV, EXPERTS, TOP, CAP, 2))(routes_keys, routes_turns).reshape((TOKENS, TOP))
    combine = jnp.clip(0.05 + 0.35 * jax.random.uniform(key_list[3], (TOKENS, TOP), jnp.float32) ** level_of(key_list[3], (TOKENS, TOP), ((0, 64),), -0.2, 0.2), 0.05, 0.4)
    w_gate = scatter_about(key_list[4], (EXPERTS, D, FF), D ** -0.5, 0.09375, ((0, 64), (1, 16)))
    w_up = scatter_about(key_list[5], (EXPERTS, D, FF), D ** -0.5, 0.09375, ((0, 64), (1, 16)))
    w_down = scatter_about(key_list[6], (EXPERTS, FF, D), FF ** -0.5, 0.21875, ((0, 64), (2, 16)))
    return dict(acts=acts, grad_out=grad_out, routes=routes, combine=combine, w_gate=w_gate, w_up=w_up, w_down=w_down)


def activate(pre_gate, pre_up, hidden_grad):
    sigmoid_gate = jax.nn.sigmoid(pre_gate)
    silu_gate = pre_gate * sigmoid_gate
    hidden = (silu_gate * pre_up).astype(jnp.bfloat16)
    up_grad = (hidden_grad * silu_gate).astype(jnp.bfloat16)
    gate_grad = (hidden_grad * pre_up * sigmoid_gate * (1.0 + pre_gate * (1.0 - sigmoid_gate))).astype(jnp.bfloat16)
    return hidden, gate_grad, up_grad


def reference(acts, grad_out, routes, combine, w_gate, w_up, w_down):
    pick_total = TOKENS * TOP
    flat_ids = routes.reshape(-1).astype(jnp.int32)
    owner = (jnp.arange(pick_total, dtype=jnp.int32) // TOP).astype(jnp.int32)
    onehot = (flat_ids[:, None] == jnp.arange(EXPERTS, dtype=jnp.int32)[None, :]).astype(jnp.int32)
    ranking = jnp.sum((jnp.cumsum(onehot, axis=0) - 1) * onehot, axis=1).astype(jnp.int32)
    scaled = (combine[:, :, None] * grad_out[:, None, :].astype(jnp.float32)).astype(jnp.bfloat16).reshape(pick_total, D)

    def one_expert(expert_id):
        chosen = flat_ids == expert_id
        target = jnp.where(chosen, ranking, ROWS).astype(jnp.int32)
        source = jnp.full((ROWS + 1,), pick_total, jnp.int32).at[target].set(jnp.arange(pick_total, dtype=jnp.int32))[:ROWS]
        valid = source < pick_total
        safe_src = jnp.minimum(source, pick_total - 1).astype(jnp.int32)
        rows_x = jnp.where(valid[:, None], acts[owner[safe_src]], jnp.zeros((), jnp.bfloat16)).astype(jnp.bfloat16)
        rows_dy = jnp.where(valid[:, None], scaled[safe_src], jnp.zeros((), jnp.bfloat16)).astype(jnp.bfloat16)
        gate_w = w_gate[expert_id]
        up_w = w_up[expert_id]
        down_w = w_down[expert_id]
        pre_gate = jnp.dot(rows_x, gate_w, preferred_element_type=jnp.float32)
        pre_up = jnp.dot(rows_x, up_w, preferred_element_type=jnp.float32)
        hidden_grad = jnp.dot(rows_dy, down_w.T, preferred_element_type=jnp.float32)
        hidden, gate_grad, up_grad = activate(pre_gate, pre_up, hidden_grad)
        grad_gate = jnp.dot(rows_x.T, gate_grad, preferred_element_type=jnp.float32).astype(jnp.bfloat16)
        grad_up = jnp.dot(rows_x.T, up_grad, preferred_element_type=jnp.float32).astype(jnp.bfloat16)
        grad_down = jnp.dot(hidden.T, rows_dy, preferred_element_type=jnp.float32).astype(jnp.bfloat16)
        row_grad = (jnp.dot(gate_grad, gate_w.T, preferred_element_type=jnp.float32) + jnp.dot(up_grad, up_w.T, preferred_element_type=jnp.float32)).astype(jnp.bfloat16)
        return grad_gate, grad_up, grad_down, row_grad

    grad_gate_w, grad_up_w, grad_down_w, row_grads = lax.map(one_expert, jnp.arange(EXPERTS, dtype=jnp.int32))
    per_pick = row_grads[flat_ids, ranking].astype(jnp.float32).reshape(TOKENS, TOP, D)
    grad_acts = jnp.sum(per_pick, axis=1).astype(jnp.bfloat16)
    return grad_acts, grad_gate_w, grad_up_w, grad_down_w
```

```python
import functools

import jax
import jax.numpy as jnp
from jax import lax
from jax.experimental import pallas as pl
from jax.experimental.pallas import tpu as pltpu
from jax.sharding import PartitionSpec as P

BF16 = jnp.bfloat16
F32 = jnp.float32
TOK = 16
PICKS = 8
EXPERTS = 64
CAP = 3
ROWS = EXPERTS * CAP
WIDTH = 256
HIDDEN = 768
HALF = HIDDEN // 2
PACK = 3 * HALF
GROUP = 4
CHUNK = 24
NEAR = [[GROUP * a + b for b in range(GROUP)] for a in range(GROUP)]
FAR = [[GROUP * a + b for a in range(GROUP)] for b in range(GROUP)]
VMEM_LIMIT = 24 * 1024 * 1024


def dot(a, b, contract):
    return lax.dot_general(a, b, (contract, ((), ())), preferred_element_type=F32)


def iota(shape, dim):
    return lax.broadcasted_iota(jnp.int32, shape, dim)


def column(row):
    diagonal = iota((TOK, TOK), 0) == iota((TOK, TOK), 1)
    spread = jnp.where(diagonal, jnp.broadcast_to(row, (TOK, TOK)), jnp.zeros((), row.dtype))
    return jnp.sum(spread, axis=1, keepdims=True)


def slots_of(routes_t):
    expert = lax.shift_right_logical(iota((TOK, EXPERTS * 8), 1), 3)
    hits = [column(routes_t[k : k + 1, :]) == expert for k in range(PICKS)]
    named = functools.reduce(jnp.logical_or, hits)
    earlier = (iota((TOK, TOK), 0) > iota((TOK, TOK), 1)).astype(F32).astype(BF16)
    rank = dot(earlier, named.astype(F32).astype(BF16), ((1,), (0,))).astype(jnp.int32)
    return hits, named, rank


def as_bf16(mask):
    return mask.astype(F32).astype(BF16)


def dispatch_body(routes_t, combine_t, acts, grad_out):
    hits, named, rank = slots_of(routes_t)
    place = jnp.bitwise_and(iota((TOK, EXPERTS * 8), 1), 7)
    wanted_x = place == rank
    wanted_dy = place == rank + 4
    choose = [as_bf16(named & wanted_x)] + [as_bf16(hit & wanted_dy) for hit in hits]
    wide = grad_out.astype(F32)
    values = [acts] + [(column(combine_t[k : k + 1, :]) * wide).astype(BF16) for k in range(PICKS)]
    choose = jnp.concatenate(choose, axis=0)
    values = jnp.concatenate(values, axis=0)
    return dot(choose, values, ((0,), (0,))).astype(BF16)


def dispatch_kernel(routes_ref, combine_ref, acts_ref, grad_ref, out_ref):
    out_ref[...] = dispatch_body(routes_ref[...], combine_ref[...], acts_ref[...], grad_ref[...])


def rows_body(received):
    row, slot = iota((ROWS, EXPERTS * 8), 0), iota((ROWS, EXPERTS * 8), 1)
    base = jnp.bitwise_and(row, EXPERTS - 1) * 8 + lax.shift_right_logical(row, 6)
    rows_x = dot(as_bf16(slot == base), received, ((1,), (0,))).astype(BF16)
    rows_dy = dot(as_bf16(slot == base + 4), received, ((1,), (0,))).astype(BF16)
    return rows_x, rows_dy


def product_blocks(rows_x, rows_dy, w_gate, w_up, w_down):
    gate = dot(rows_x, w_gate, ((1,), (0,)))
    up = dot(rows_x, w_up, ((1,), (0,)))
    back = dot(rows_dy, w_down, ((1,), (1,)))
    blocks = {}
    for half in range(2):
        cut = slice(half * HALF, (half + 1) * HALF)
        both = jnp.concatenate([gate[:, cut], up[:, cut], back[:, cut]], axis=1)
        for b in range(GROUP):
            low, high = CHUNK * b, CHUNK * (GROUP + b)
            block = jnp.concatenate([both[low : low + CHUNK], both[high : high + CHUNK]], axis=0)
            blocks[b, half] = block.astype(BF16)
    return blocks


def product_kernel(received_ref, w_gate_ref, w_up_ref, w_down_ref, parts_ref, x_ref, dy_ref):
    rows_x, rows_dy = rows_body(received_ref[...])
    x_ref[...] = rows_x
    dy_ref[...] = rows_dy
    blocks = product_blocks(rows_x, rows_dy, w_gate_ref[...], w_up_ref[...], w_down_ref[...])
    for (b, half), block in blocks.items():
        parts_ref[b, 2 * CHUNK * half : 2 * CHUNK * (half + 1), :] = block


def add_body(parts):
    return (parts[0].astype(F32) + parts[1].astype(F32)) + (parts[2].astype(F32) + parts[3].astype(F32))


def add_kernel(parts_ref, out_ref):
    out_ref[...] = add_body(parts_ref[...]).astype(BF16)


def activate_body(parts):
    total = add_body(parts)
    pre_gate, pre_up, hidden_grad = total[:, :HALF], total[:, HALF : 2 * HALF], total[:, 2 * HALF :]
    sigmoid_gate = jax.nn.sigmoid(pre_gate)
    silu_gate = pre_gate * sigmoid_gate
    hidden = silu_gate * pre_up
    up_grad = hidden_grad * silu_gate
    gate_grad = hidden_grad * pre_up * sigmoid_gate * (1.0 + pre_gate * (1.0 - sigmoid_gate))
    return jnp.concatenate([gate_grad, up_grad, hidden], axis=1).astype(BF16)


def activate_kernel(parts_ref, out_ref):
    out_ref[...] = activate_body(parts_ref[...])


def row_grad_body(packed, w_gate, w_up):
    total = jnp.zeros((ROWS, WIDTH), F32)
    for half in range(2):
        cut = slice(half * HALF, (half + 1) * HALF)
        total += dot(packed[half][:, :HALF], w_gate[:, cut], ((1,), (1,)))
        total += dot(packed[half][:, HALF : 2 * HALF], w_up[:, cut], ((1,), (1,)))
    rounded = total.astype(BF16)
    slot, row = iota((EXPERTS * 8, ROWS), 0), iota((EXPERTS * 8, ROWS), 1)
    base = jnp.bitwise_and(row, EXPERTS - 1) * 8 + lax.shift_right_logical(row, 6) * 2
    left = dot(as_bf16(slot == base), rounded[:, :128], ((1,), (0,)))
    right = dot(as_bf16(slot == base + 1), rounded[:, 128:], ((1,), (0,)))
    return (left + right).astype(BF16)


def row_grad_kernel(packed_ref, w_gate_ref, w_up_ref, out_ref):
    out_ref[...] = row_grad_body(packed_ref[...], w_gate_ref[...], w_up_ref[...])


def weight_kernel(packed_ref, x_ref, dy_ref, gate_ref, up_ref, down_ref):
    rows_x, rows_dy = x_ref[...], dy_ref[...]
    for half in range(2):
        cut = slice(half * HALF, (half + 1) * HALF)
        gate_ref[:, cut] = dot(rows_x, packed_ref[half, :, :HALF], ((0,), (0,))).astype(BF16)
        up_ref[:, cut] = dot(rows_x, packed_ref[half, :, HALF : 2 * HALF], ((0,), (0,))).astype(BF16)
        down_ref[cut, :] = dot(packed_ref[half, :, 2 * HALF :], rows_dy, ((0,), (0,))).astype(BF16)


def combine_body(routes_t, returned):
    _, named, rank = slots_of(routes_t)
    place = jnp.bitwise_and(iota((TOK, EXPERTS * 8), 1), 7)
    left = dot(as_bf16(named & (place == 2 * rank)), returned, ((1,), (0,)))
    right = dot(as_bf16(named & (place == 2 * rank + 1)), returned, ((1,), (0,)))
    return jnp.concatenate([left, right], axis=1).astype(BF16)


def combine_kernel(routes_ref, returned_ref, out_ref):
    out_ref[...] = combine_body(routes_ref[...], returned_ref[...])


def call(kernel, outs, flops, *operands):
    shapes = [jax.ShapeDtypeStruct(shape, BF16) for shape in outs]
    moved = sum(x.size * x.dtype.itemsize for x in operands) + sum(2 * s.size for s in shapes)
    return pl.pallas_call(
        kernel,
        out_shape=shapes if len(shapes) > 1 else shapes[0],
        cost_estimate=pl.CostEstimate(flops=flops, bytes_accessed=moved, transcendentals=0),
        compiler_params=pltpu.CompilerParams(vmem_limit_bytes=VMEM_LIMIT),
    )(*operands)


def on_device(acts, grad_out, routes, combine, w_gate, w_up, w_down):
    gate_w, up_w, down_w = w_gate[0], w_up[0], w_down[0]
    slots = EXPERTS * 8
    matmul = 2 * ROWS * WIDTH * HIDDEN

    sent = call(dispatch_kernel, [(slots, WIDTH)], 2 * slots * 144 * WIDTH, routes.T, combine.T, acts, grad_out)
    received = lax.all_to_all(sent.reshape(EXPERTS, 8, WIDTH), "expert", 0, 0, tiled=True)

    parts, rows_x, rows_dy = call(
        product_kernel,
        [(GROUP, 4 * CHUNK, PACK), (ROWS, WIDTH), (ROWS, WIDTH)],
        3 * matmul,
        received.reshape(slots, WIDTH),
        gate_w,
        up_w,
        down_w,
    )
    parts = lax.all_to_all(parts, "dp", 0, 0, tiled=True, axis_index_groups=NEAR)
    parts = call(add_kernel, [(4 * CHUNK, PACK)], 4 * 4 * CHUNK * PACK, parts)
    parts = lax.all_to_all(
        parts.reshape(GROUP, CHUNK, PACK), "dp", 0, 0, tiled=True, axis_index_groups=FAR
    )
    block = call(activate_kernel, [(CHUNK, PACK)], 20 * CHUNK * PACK, parts)
    packed = lax.all_gather(block, "dp", axis=0).reshape(2, ROWS, PACK)

    row_grads = call(row_grad_kernel, [(slots, 128)], 2 * matmul, packed, gate_w, up_w)
    returned = lax.all_to_all(row_grads.reshape(EXPERTS, 8, 128), "expert", 0, 0, tiled=True)
    new_gate, new_up, new_down = call(
        weight_kernel,
        [(WIDTH, HIDDEN), (WIDTH, HIDDEN), (HIDDEN, WIDTH)],
        3 * matmul,
        packed,
        rows_x,
        rows_dy,
    )
    grad_acts = call(
        combine_kernel, [(TOK, WIDTH)], 4 * TOK * slots * 128, routes.T, returned.reshape(slots, 128)
    )
    return grad_acts, new_gate[None], new_up[None], new_down[None]


def solution(mesh):
    return jax.shard_map(
        on_device,
        mesh=mesh,
        in_specs=(
            P("expert", "dp"),
            P("expert", "dp"),
            P("expert", None),
            P("expert", None),
            P("expert", "dp", None),
            P("expert", "dp", None),
            P("expert", None, "dp"),
        ),
        out_specs=(
            P("expert", "dp"),
            P("expert", "dp", None),
            P("expert", "dp", None),
            P("expert", None, "dp"),
        ),
        check_vma=False,
    )
```

```python
import functools

import jax
import jax.numpy as jnp
from jax import lax
from jax.experimental import pallas as pl
from jax.experimental.pallas import tpu as pltpu
from jax.sharding import PartitionSpec as P

BF16 = jnp.bfloat16
F32 = jnp.float32
TOK = 16
PICKS = 8
EXPERTS = 64
CAP = 3
ROWS = EXPERTS * CAP
WIDTH = 256
HIDDEN = 768
HALF = HIDDEN // 2
PACK = 3 * HALF
CHUNK = 24
DP = 16
SLOTS = EXPERTS * 8
SAME_PARITY = [[2 * a + b for a in range(DP // 2)] for b in range(2)]
VMEM_LIMIT = 24 * 1024 * 1024


def dot(a, b, contract):
    return lax.dot_general(a, b, (contract, ((), ())), preferred_element_type=F32)


def iota(shape, dim):
    return lax.broadcasted_iota(jnp.int32, shape, dim)


def column(row):
    diagonal = iota((TOK, TOK), 0) == iota((TOK, TOK), 1)
    spread = jnp.where(diagonal, jnp.broadcast_to(row, (TOK, TOK)), jnp.zeros((), row.dtype))
    return jnp.sum(spread, axis=1, keepdims=True)


def slots_of(routes_t):
    expert = lax.shift_right_logical(iota((TOK, SLOTS), 1), 3)
    hits = [column(routes_t[k : k + 1, :]) == expert for k in range(PICKS)]
    named = functools.reduce(jnp.logical_or, hits)
    earlier = (iota((TOK, TOK), 0) > iota((TOK, TOK), 1)).astype(F32).astype(BF16)
    rank = dot(earlier, named.astype(F32).astype(BF16), ((1,), (0,))).astype(jnp.int32)
    return hits, named, rank


def as_bf16(mask):
    return mask.astype(F32).astype(BF16)


def dispatch_body(routes_t, combine_t, acts, grad_out):
    hits, named, rank = slots_of(routes_t)
    place = jnp.bitwise_and(iota((TOK, SLOTS), 1), 7)
    wanted_x = place == rank
    wanted_dy = place == rank + 4
    choose = [as_bf16(named & wanted_x)] + [as_bf16(hit & wanted_dy) for hit in hits]
    wide = grad_out.astype(F32)
    values = [acts] + [(column(combine_t[k : k + 1, :]) * wide).astype(BF16) for k in range(PICKS)]
    sent = dot(jnp.concatenate(choose, axis=0), jnp.concatenate(values, axis=0), ((0,), (0,)))
    back = [as_bf16(named & (place == 2 * rank + half)) for half in range(2)]
    return sent.astype(BF16), jnp.concatenate(back, axis=0)


def dispatch_kernel(routes, combine, acts, grad_out, sent_ref, back_ref, *scratch):
    held, arrived = scratch[:4], scratch[4]
    copies = [
        pltpu.make_async_copy(source, place, arrived.at[i])
        for i, (source, place) in enumerate(zip((routes, combine, acts, grad_out), held))
    ]
    for copy in copies:
        copy.start()
    for copy in copies:
        copy.wait()
    sent_ref[...], back_ref[...] = dispatch_body(*(place[...] for place in held))


def take_rows(received, row):
    base = jnp.bitwise_and(row, EXPERTS - 1) * 8 + lax.shift_right_logical(row, 6)
    slot = iota((ROWS, SLOTS), 1)
    rows_x = dot(as_bf16(slot == base), received, ((1,), (0,))).astype(BF16)
    rows_dy = dot(as_bf16(slot == base + 4), received, ((1,), (0,))).astype(BF16)
    return rows_x, rows_dy


def own_rows_first(parity):
    place = iota((ROWS, 1), 0)
    second = (place >= ROWS // 2).astype(jnp.int32)
    within = place - second * (ROWS // 2)
    chunk = sum((within >= CHUNK * i).astype(jnp.int32) for i in range(1, 4))
    return within + CHUNK * chunk + CHUNK * jnp.bitwise_xor(second, parity)


def products(rows_x, rows_dy, w_gate, w_up, w_down):
    gate = dot(rows_x, w_gate, ((1,), (0,)))
    up = dot(rows_x, w_up, ((1,), (0,)))
    back = dot(rows_dy, w_down(), ((1,), (1,)))
    cuts = [slice(half * HALF, (half + 1) * HALF) for half in range(2)]
    return [jnp.concatenate([gate[:, cut], up[:, cut], back[:, cut]], axis=1) for cut in cuts]


def product_kernel(received_ref, w_gate_ref, w_up_ref, w_down, own_ref, send_ref, down_ref, arrived):
    copy = pltpu.make_async_copy(w_down, down_ref, arrived)
    copy.start()

    def held():
        copy.wait()
        return down_ref[...]

    parity = jnp.bitwise_and(lax.axis_index("dp"), 1)
    rows_x, rows_dy = take_rows(received_ref[...], own_rows_first(parity))
    halves = products(rows_x, rows_dy, w_gate_ref[...], w_up_ref[...], held)
    for half, both in enumerate(halves):
        own_ref[half] = both[: ROWS // 2]
        send_ref[half] = both[ROWS // 2 :].astype(BF16)


def pair_body(own, taken):
    return (own + taken.astype(F32)).astype(BF16)


def pair_kernel(own_ref, taken_ref, out_ref):
    out_ref[...] = pair_body(own_ref[...], taken_ref[...])


def activate_body(parts):
    total = [parts[i].astype(F32) for i in range(8)]
    while len(total) > 1:
        total = [total[i] + total[i + 1] for i in range(0, len(total), 2)]
    total = total[0]
    pre_gate, pre_up, hidden_grad = total[:, :HALF], total[:, HALF : 2 * HALF], total[:, 2 * HALF :]
    sigmoid_gate = jax.nn.sigmoid(pre_gate)
    silu_gate = pre_gate * sigmoid_gate
    hidden = silu_gate * pre_up
    up_grad = hidden_grad * silu_gate
    gate_grad = hidden_grad * pre_up * sigmoid_gate * (1.0 + pre_gate * (1.0 - sigmoid_gate))
    return jnp.concatenate([gate_grad, up_grad, hidden], axis=1).astype(BF16)


def activate_kernel(parts_ref, out_ref):
    out_ref[...] = activate_body(parts_ref[...])


def row_grad_body(packed, w_gate, w_up):
    total = jnp.zeros((ROWS, WIDTH), F32)
    for half in range(2):
        cut = slice(half * HALF, (half + 1) * HALF)
        total += dot(packed[half][:, :HALF], w_gate[:, cut], ((1,), (1,)))
        total += dot(packed[half][:, HALF : 2 * HALF], w_up[:, cut], ((1,), (1,)))
    rounded = total.astype(BF16)
    slot, row = iota((SLOTS, ROWS), 0), iota((1, ROWS), 1)
    base = jnp.bitwise_and(row, EXPERTS - 1) * 8 + lax.shift_right_logical(row, 6) * 2
    left = dot(as_bf16(slot == base), rounded[:, :128], ((1,), (0,)))
    right = dot(as_bf16(slot == base + 1), rounded[:, 128:], ((1,), (0,)))
    return (left + right).astype(BF16)


def row_grad_kernel(packed_ref, w_gate_ref, w_up_ref, out_ref):
    out_ref[...] = row_grad_body(packed_ref[...], w_gate_ref[...], w_up_ref[...])


def weight_kernel(packed_ref, received_ref, gate_ref, up_ref, down_ref):
    rows_x, rows_dy = take_rows(received_ref[...], iota((ROWS, 1), 0))
    for half in range(2):
        cut = slice(half * HALF, (half + 1) * HALF)
        gate_ref[:, cut] = dot(rows_x, packed_ref[half, :, :HALF], ((0,), (0,))).astype(BF16)
        up_ref[:, cut] = dot(rows_x, packed_ref[half, :, HALF : 2 * HALF], ((0,), (0,))).astype(BF16)
        down_ref[cut, :] = dot(packed_ref[half, :, 2 * HALF :], rows_dy, ((0,), (0,))).astype(BF16)


def combine_body(back, returned):
    left = dot(back[:TOK], returned, ((1,), (0,)))
    right = dot(back[TOK:], returned, ((1,), (0,)))
    return jnp.concatenate([left, right], axis=1).astype(BF16)


def combine_kernel(back_ref, returned_ref, out_ref):
    out_ref[...] = combine_body(back_ref[...], returned_ref[...])


def call(kernel, outs, flops, *operands, **options):
    shapes = [jax.ShapeDtypeStruct(shape, dtype) for shape, dtype in outs]
    moved = sum(x.size * x.dtype.itemsize for x in [*operands, *shapes])
    return pl.pallas_call(
        kernel,
        out_shape=shapes if len(shapes) > 1 else shapes[0],
        cost_estimate=pl.CostEstimate(flops=flops, bytes_accessed=moved, transcendentals=0),
        compiler_params=pltpu.CompilerParams(vmem_limit_bytes=VMEM_LIMIT),
        **options,
    )(*operands)


ANY = pl.BlockSpec(memory_space=pl.ANY)
VMEM = pl.BlockSpec(memory_space=pltpu.VMEM)


def on_device(acts, grad_out, routes, combine, w_gate, w_up, w_down):
    gate_w, up_w, down_w = w_gate[0], w_up[0], w_down[0]
    matmul = 2 * ROWS * WIDTH * HIDDEN

    sent, back = call(
        dispatch_kernel,
        [((SLOTS, WIDTH), BF16), ((2 * TOK, SLOTS), BF16)],
        2 * SLOTS * 144 * WIDTH,
        routes.T,
        combine.T,
        acts,
        grad_out,
        in_specs=[ANY] * 4,
        scratch_shapes=[
            pltpu.VMEM((PICKS, TOK), jnp.int32),
            pltpu.VMEM((PICKS, TOK), F32),
            pltpu.VMEM((TOK, WIDTH), BF16),
            pltpu.VMEM((TOK, WIDTH), BF16),
            pltpu.SemaphoreType.DMA((4,)),
        ],
    )
    received = lax.all_to_all(sent.reshape(EXPERTS, 8, WIDTH), "expert", 0, 0, tiled=True)
    received = received.reshape(SLOTS, WIDTH)

    own, send = call(
        product_kernel,
        [((2, ROWS // 2, PACK), F32), ((2, ROWS // 2, PACK), BF16)],
        3 * matmul,
        received,
        gate_w,
        up_w,
        down_w,
        in_specs=[VMEM, VMEM, VMEM, ANY],
        scratch_shapes=[pltpu.VMEM((HIDDEN, WIDTH), BF16), pltpu.SemaphoreType.DMA(())],
    )
    taken = lax.ppermute(send, "dp", [(i, i ^ 1) for i in range(DP)])
    parts = call(pair_kernel, [((2, ROWS // 2, PACK), BF16)], ROWS * PACK, own, taken)
    parts = lax.all_to_all(
        parts.reshape(DP // 2, CHUNK, PACK), "dp", 0, 0, tiled=True, axis_index_groups=SAME_PARITY
    )
    block = call(activate_kernel, [((CHUNK, PACK), BF16)], 20 * CHUNK * PACK, parts)
    packed = lax.all_gather(block, "dp", axis=0).reshape(2, ROWS, PACK)

    row_grads = call(row_grad_kernel, [((SLOTS, 128), BF16)], 2 * matmul, packed, gate_w, up_w)
    returned = lax.all_to_all(row_grads.reshape(EXPERTS, 8, 128), "expert", 0, 0, tiled=True)
    new_gate, new_up, new_down = call(
        weight_kernel,
        [((WIDTH, HIDDEN), BF16), ((WIDTH, HIDDEN), BF16), ((HIDDEN, WIDTH), BF16)],
        3 * matmul,
        packed,
        received,
    )
    grad_acts = call(
        combine_kernel, [((TOK, WIDTH), BF16)], 4 * TOK * SLOTS * 128, back, returned.reshape(SLOTS, 128)
    )
    return grad_acts, new_gate[None], new_up[None], new_down[None]


def solution(mesh):
    return jax.shard_map(
        on_device,
        mesh=mesh,
        in_specs=(
            P("expert", "dp"),
            P("expert", "dp"),
            P("expert", None),
            P("expert", None),
            P("expert", "dp", None),
            P("expert", "dp", None),
            P("expert", None, "dp"),
        ),
        out_specs=(
            P("expert", "dp"),
            P("expert", "dp", None),
            P("expert", "dp", None),
            P("expert", None, "dp"),
        ),
        check_vma=False,
    )
```

```python
import functools

import jax
import jax.numpy as jnp
from jax import lax
from jax.experimental import pallas as pl
from jax.experimental.pallas import tpu as pltpu
from jax.sharding import PartitionSpec as P

BF16 = jnp.bfloat16
F32 = jnp.float32
TOK = 16
PICKS = 8
EXPERTS = 64
CAP = 3
ROWS = EXPERTS * CAP
WIDTH = 256
HIDDEN = 768
HALF = HIDDEN // 2
PACK = 3 * HALF
CHUNK = 24
DP = 16
SLOTS = EXPERTS * 8
SAME_PARITY = [[2 * a + b for a in range(DP // 2)] for b in range(2)]
def partner(dp, expert):
    if expert % 2 == 0:
        return dp ^ 1
    return (dp + 1) % DP if dp % 2 else (dp - 1) % DP


PAIRS = [
    (dp * EXPERTS + expert, partner(dp, expert) * EXPERTS + expert) for dp in range(DP) for expert in range(EXPERTS)
]
VMEM_LIMIT = 24 * 1024 * 1024


def dot(a, b, contract):
    return lax.dot_general(a, b, (contract, ((), ())), preferred_element_type=F32)


def iota(shape, dim):
    return lax.broadcasted_iota(jnp.int32, shape, dim)


def column(row):
    diagonal = iota((TOK, TOK), 0) == iota((TOK, TOK), 1)
    spread = jnp.where(diagonal, jnp.broadcast_to(row, (TOK, TOK)), jnp.zeros((), row.dtype))
    return jnp.sum(spread, axis=1, keepdims=True)


def slots_of(routes_t):
    expert = lax.shift_right_logical(iota((TOK, SLOTS), 1), 3)
    hits = [column(routes_t[k : k + 1, :]) == expert for k in range(PICKS)]
    named = functools.reduce(jnp.logical_or, hits)
    earlier = (iota((TOK, TOK), 0) > iota((TOK, TOK), 1)).astype(F32).astype(BF16)
    rank = dot(earlier, named.astype(F32).astype(BF16), ((1,), (0,))).astype(jnp.int32)
    return hits, named, rank


def as_bf16(mask):
    return mask.astype(F32).astype(BF16)


def dispatch_body(routes_t, combine_t, acts, grad_out):
    hits, named, rank = slots_of(routes_t)
    place = jnp.bitwise_and(iota((TOK, SLOTS), 1), 7)
    wanted_x = place == rank
    wanted_dy = place == rank + 4
    choose = [as_bf16(named & wanted_x)] + [as_bf16(hit & wanted_dy) for hit in hits]
    wide = grad_out.astype(F32)
    values = [acts] + [(column(combine_t[k : k + 1, :]) * wide).astype(BF16) for k in range(PICKS)]
    sent = dot(jnp.concatenate(choose, axis=0), jnp.concatenate(values, axis=0), ((0,), (0,)))
    back = [as_bf16(named & (place == 2 * rank + half)) for half in range(2)]
    return sent.astype(BF16), jnp.concatenate(back, axis=0)


def dispatch_kernel(routes, combine, acts, grad_out, sent_ref, back_ref, *scratch):
    held, arrived = scratch[:4], scratch[4]
    copies = [
        pltpu.make_async_copy(source, place, arrived.at[i])
        for i, (source, place) in enumerate(zip((routes, combine, acts, grad_out), held))
    ]
    for copy in copies:
        copy.start()
    for copy in copies:
        copy.wait()
    sent_ref[...], back_ref[...] = dispatch_body(*(place[...] for place in held))


def take_rows(received_ref, held):
    parts = []
    for half in range(2):
        held[half] = received_ref[:, 128 * half : 128 * (half + 1)].astype(F32)
        parts.append([held[half, pl.Slice(place, EXPERTS, 8), :] for place in range(7)])
    full = [jnp.concatenate(pair, axis=1).astype(BF16) for pair in zip(*parts)]
    return jnp.concatenate(full[:CAP], axis=0), jnp.concatenate(full[4 : 4 + CAP], axis=0)


def products(rows_x, rows_dy, w_gate, w_up, w_down):
    gate = dot(rows_x, w_gate, ((1,), (0,)))
    up = dot(rows_x, w_up, ((1,), (0,)))
    back = dot(rows_dy, w_down, ((1,), (1,)))
    cuts = [slice(half * HALF, (half + 1) * HALF) for half in range(2)]
    return [jnp.concatenate([gate[:, cut], up[:, cut], back[:, cut]], axis=1) for cut in cuts]


def split_rows(both, parity):
    even, odd = (
        jnp.concatenate([both[CHUNK * i : CHUNK * (i + 1)] for i in range(first, 8, 2)], axis=0)
        for first in range(2)
    )
    is_odd = parity == 1
    return jnp.where(is_odd, odd, even), jnp.where(is_odd, even, odd)


def product_kernel(received_ref, w_gate_ref, w_up_ref, w_down_ref, own_ref, send_ref, held):
    rows_x, rows_dy = take_rows(received_ref, held)
    parity = jnp.bitwise_and(lax.axis_index("dp"), 1)
    for half, both in enumerate(products(rows_x, rows_dy, w_gate_ref[...], w_up_ref[...], w_down_ref[...])):
        own, other = split_rows(both, parity)
        own_ref[half] = own
        send_ref[half] = other.astype(BF16)


def pair_kernel(own_ref, taken_ref, out_ref, left_ref):
    total = own_ref[...] + taken_ref[...].astype(F32)
    out_ref[...] = total.astype(BF16)
    mine = lax.shift_right_logical(lax.axis_index("dp"), 1)
    kept = own_ref[mine] + taken_ref[mine].astype(F32)
    left_ref[...] = kept - kept.astype(BF16).astype(F32)


def activate_body(parts, left):
    total = [parts[i].astype(F32) for i in range(8)]
    while len(total) > 1:
        total = [total[i] + total[i + 1] for i in range(0, len(total), 2)]
    total = total[0] + left
    pre_gate, pre_up, hidden_grad = total[:, :HALF], total[:, HALF : 2 * HALF], total[:, 2 * HALF :]
    sigmoid_gate = jax.nn.sigmoid(pre_gate)
    silu_gate = pre_gate * sigmoid_gate
    hidden = silu_gate * pre_up
    up_grad = hidden_grad * silu_gate
    gate_grad = hidden_grad * pre_up * sigmoid_gate * (1.0 + pre_gate * (1.0 - sigmoid_gate))
    return jnp.concatenate([gate_grad, up_grad, hidden], axis=1).astype(BF16)


def activate_kernel(parts_ref, left_ref, out_ref):
    out_ref[...] = activate_body(parts_ref[...], left_ref[...])


def row_grad_body(packed, w_gate, w_up):
    total = jnp.zeros((ROWS, WIDTH), F32)
    for half in range(2):
        cut = slice(half * HALF, (half + 1) * HALF)
        total += dot(packed[half][:, :HALF], w_gate[:, cut], ((1,), (1,)))
        total += dot(packed[half][:, HALF : 2 * HALF], w_up[:, cut], ((1,), (1,)))
    return total


def row_grad_kernel(packed_ref, w_gate_ref, w_up_ref, out_ref, held):
    total = row_grad_body(packed_ref[...], w_gate_ref[...], w_up_ref[...])
    for place in range(8):
        slot, half = divmod(place, 2)
        if slot < CAP:
            value = total[EXPERTS * slot : EXPERTS * (slot + 1), 128 * half : 128 * (half + 1)]
        else:
            value = jnp.zeros((EXPERTS, 128), F32)
        held[pl.Slice(place, EXPERTS, 8), :] = value
    out_ref[...] = held[...].astype(BF16)


def weight_kernel(packed_ref, received_ref, gate_ref, up_ref, down_ref, held):
    rows_x, rows_dy = take_rows(received_ref, held)
    for half in range(2):
        cut = slice(half * HALF, (half + 1) * HALF)
        gate_ref[:, cut] = dot(rows_x, packed_ref[half, :, :HALF], ((0,), (0,))).astype(BF16)
        up_ref[:, cut] = dot(rows_x, packed_ref[half, :, HALF : 2 * HALF], ((0,), (0,))).astype(BF16)
        down_ref[cut, :] = dot(packed_ref[half, :, 2 * HALF :], rows_dy, ((0,), (0,))).astype(BF16)


def combine_body(back, returned):
    left = dot(back[:TOK], returned, ((1,), (0,)))
    right = dot(back[TOK:], returned, ((1,), (0,)))
    return jnp.concatenate([left, right], axis=1).astype(BF16)


def combine_kernel(back_ref, returned_ref, out_ref):
    out_ref[...] = combine_body(back_ref[...], returned_ref[...])


def call(kernel, outs, flops, *operands, **options):
    shapes = [jax.ShapeDtypeStruct(shape, dtype) for shape, dtype in outs]
    moved = sum(x.size * x.dtype.itemsize for x in [*operands, *shapes])
    return pl.pallas_call(
        kernel,
        out_shape=shapes if len(shapes) > 1 else shapes[0],
        cost_estimate=pl.CostEstimate(flops=flops, bytes_accessed=moved, transcendentals=0),
        compiler_params=pltpu.CompilerParams(vmem_limit_bytes=VMEM_LIMIT),
        **options,
    )(*operands)


HBM = pl.BlockSpec(memory_space=pltpu.HBM)
TAKEN = pltpu.VMEM((2, SLOTS, 128), F32)


def on_device(acts, grad_out, routes, combine, w_gate, w_up, w_down):
    gate_w, up_w, down_w = w_gate[0], w_up[0], w_down[0]
    matmul = 2 * ROWS * WIDTH * HIDDEN

    sent, back = call(
        dispatch_kernel,
        [((SLOTS, WIDTH), BF16), ((2 * TOK, SLOTS), BF16)],
        4 * matmul,
        *(pltpu.with_memory_space_constraint(x, pltpu.HBM) for x in (routes.T, combine.T, acts, grad_out)),
        in_specs=[HBM] * 4,
        scratch_shapes=[
            pltpu.VMEM((PICKS, TOK), jnp.int32),
            pltpu.VMEM((PICKS, TOK), F32),
            pltpu.VMEM((TOK, WIDTH), BF16),
            pltpu.VMEM((TOK, WIDTH), BF16),
            pltpu.SemaphoreType.DMA((4,)),
        ],
    )
    received = lax.all_to_all(sent.reshape(EXPERTS, 8, WIDTH), "expert", 0, 0, tiled=True)
    received = received.reshape(SLOTS, WIDTH)

    own, send = call(
        product_kernel,
        [((2, ROWS // 2, PACK), F32), ((2, ROWS // 2, PACK), BF16)],
        3 * matmul,
        received,
        gate_w,
        up_w,
        down_w,
        scratch_shapes=[TAKEN],
    )
    taken = lax.ppermute(send, ("dp", "expert"), PAIRS)
    eighths = (DP // 2, CHUNK, PACK)
    parts, left = call(
        pair_kernel,
        [(eighths, BF16), ((CHUNK, PACK), F32)],
        ROWS * PACK,
        own.reshape(eighths),
        taken.reshape(eighths),
    )
    parts = lax.all_to_all(parts, "dp", 0, 0, tiled=True, axis_index_groups=SAME_PARITY)
    block = call(activate_kernel, [((CHUNK, PACK), BF16)], 20 * CHUNK * PACK, parts, left)
    packed = lax.all_gather(block, "dp", axis=0).reshape(2, ROWS, PACK)

    row_grads = call(row_grad_kernel, [((SLOTS, 128), BF16)], 2 * matmul, packed, gate_w, up_w, scratch_shapes=[pltpu.VMEM((SLOTS, 128), F32)])
    returned = lax.all_to_all(row_grads.reshape(EXPERTS, 8, 128), "expert", 0, 0, tiled=True)
    new_gate, new_up, new_down = call(
        weight_kernel,
        [((WIDTH, HIDDEN), BF16), ((WIDTH, HIDDEN), BF16), ((HIDDEN, WIDTH), BF16)],
        3 * matmul,
        packed,
        received,
        scratch_shapes=[TAKEN],
    )
    grad_acts = call(
        combine_kernel, [((TOK, WIDTH), BF16)], 4 * TOK * SLOTS * 128, back, returned.reshape(SLOTS, 128)
    )
    return grad_acts, new_gate[None], new_up[None], new_down[None]


def solution(mesh):
    return jax.shard_map(
        on_device,
        mesh=mesh,
        in_specs=(
            P("expert", "dp"),
            P("expert", "dp"),
            P("expert", None),
            P("expert", None),
            P("expert", "dp", None),
            P("expert", "dp", None),
            P("expert", None, "dp"),
        ),
        out_specs=(
            P("expert", "dp"),
            P("expert", "dp", None),
            P("expert", "dp", None),
            P("expert", None, "dp"),
        ),
        check_vma=False,
    )
```

```python
import functools

import jax
import jax.numpy as jnp
from jax import lax
from jax.experimental import pallas as pl
from jax.experimental.pallas import tpu as pltpu
from jax.sharding import PartitionSpec as P

BF16 = jnp.bfloat16
F32 = jnp.float32
TOK = 16
PICKS = 8
EXPERTS = 64
CAP = 3
ROWS = EXPERTS * CAP
WIDTH = 256
HIDDEN = 768
HALF = HIDDEN // 2
PACK = 3 * HALF
CHUNK = 24
DP = 16
SLOTS = EXPERTS * 8
SAME_PARITY = [[2 * a + b for a in range(DP // 2)] for b in range(2)]
CORES = [[2 * chip, 2 * chip + 1] for chip in range(EXPERTS // 2)]
SAME_CORE = [[2 * chip + core for chip in range(EXPERTS // 2)] for core in range(2)]


def partner(dp, expert):
    if expert % 2 == 0:
        return dp ^ 1
    return (dp + 1) % DP if dp % 2 else (dp - 1) % DP


PAIRS = [
    [dp * EXPERTS + expert, partner(dp, expert) * EXPERTS + expert]
    for expert in range(EXPERTS)
    for dp in range(0, DP, 2)
]
VMEM_LIMIT = 24 * 1024 * 1024


def dot(a, b, contract):
    return lax.dot_general(a, b, (contract, ((), ())), preferred_element_type=F32)


def iota(shape, dim):
    return lax.broadcasted_iota(jnp.int32, shape, dim)


def column(row):
    diagonal = iota((TOK, TOK), 0) == iota((TOK, TOK), 1)
    spread = jnp.where(diagonal, jnp.broadcast_to(row, (TOK, TOK)), jnp.zeros((), row.dtype))
    return jnp.sum(spread, axis=1, keepdims=True)


def slots_of(routes_t):
    expert = lax.shift_right_logical(iota((TOK, SLOTS), 1), 3)
    hits = [column(routes_t[k : k + 1, :]) == expert for k in range(PICKS)]
    named = functools.reduce(jnp.logical_or, hits)
    earlier = (iota((TOK, TOK), 0) > iota((TOK, TOK), 1)).astype(F32).astype(BF16)
    rank = dot(earlier, named.astype(F32).astype(BF16), ((1,), (0,))).astype(jnp.int32)
    return hits, named, rank


def as_bf16(mask):
    return mask.astype(F32).astype(BF16)


def dispatch_body(routes_t, combine_t, acts, grad_out):
    hits, named, rank = slots_of(routes_t)
    place = jnp.bitwise_and(iota((TOK, SLOTS), 1), 7)
    wanted_x = place == rank
    wanted_dy = place == rank + 4
    choose = [as_bf16(named & wanted_x)] + [as_bf16(hit & wanted_dy) for hit in hits]
    wide = grad_out.astype(F32)
    values = [acts] + [(column(combine_t[k : k + 1, :]) * wide).astype(BF16) for k in range(PICKS)]
    sent = dot(jnp.concatenate(choose, axis=0), jnp.concatenate(values, axis=0), ((0,), (0,)))
    back = [as_bf16(named & (place == 2 * rank + half)) for half in range(2)]
    return sent, jnp.concatenate(back, axis=0)


def by_core(sent, core):
    split = sent.reshape(EXPERTS // 2, 2, 8, WIDTH)
    low, high = split[:, 0], split[:, 1]
    return jnp.where(core == 0, low, high), jnp.where(core == 0, high, low)


def dispatch_kernel(routes, combine, acts, grad_out, own_ref, other_ref, back_ref, *scratch):
    held, arrived = scratch[:4], scratch[4]
    copies = [
        pltpu.make_async_copy(source, place, arrived.at[i])
        for i, (source, place) in enumerate(zip((routes, combine, acts, grad_out), held))
    ]
    for copy in copies:
        copy.start()
    for copy in copies:
        copy.wait()
    sent, back_ref[...] = dispatch_body(*(place[...] for place in held))
    own, other = by_core(sent, jnp.bitwise_and(lax.axis_index("expert"), 1))
    own_ref[...] = own.reshape(SLOTS // 2, WIDTH).astype(BF16)
    other_ref[...] = other.reshape(SLOTS // 2, WIDTH).astype(BF16)


def join_kernel(own_ref, taken_ref, out_ref):
    first = lax.axis_index("expert") % 2 == 0
    own = own_ref[...].astype(F32)
    low = jnp.where(first, own, taken_ref[0].astype(F32)).reshape(EXPERTS // 2, 8, WIDTH)
    high = jnp.where(first, taken_ref[1].astype(F32), own).reshape(EXPERTS // 2, 8, WIDTH)
    out_ref[...] = jnp.concatenate([low, high], axis=1).reshape(SLOTS, WIDTH).astype(BF16)


def take_rows(received_ref, held):
    parts = []
    for half in range(2):
        held[half] = received_ref[:, 128 * half : 128 * (half + 1)].astype(F32)
        parts.append([held[half, pl.Slice(place, EXPERTS, 8), :] for place in range(7)])
    full = [jnp.concatenate(pair, axis=1).astype(BF16) for pair in zip(*parts)]
    return jnp.concatenate(full[:CAP], axis=0), jnp.concatenate(full[4 : 4 + CAP], axis=0)


def products(rows_x, rows_dy, w_gate, w_up, w_down):
    gate = dot(rows_x, w_gate, ((1,), (0,)))
    up = dot(rows_x, w_up, ((1,), (0,)))
    back = dot(rows_dy, w_down, ((1,), (1,)))
    cuts = [slice(half * HALF, (half + 1) * HALF) for half in range(2)]
    return [jnp.concatenate([gate[:, cut], up[:, cut], back[:, cut]], axis=1) for cut in cuts]


def split_rows(both, parity):
    even, odd = (
        jnp.concatenate([both[CHUNK * i : CHUNK * (i + 1)] for i in range(first, 8, 2)], axis=0)
        for first in range(2)
    )
    is_odd = parity == 1
    return jnp.where(is_odd, odd, even), jnp.where(is_odd, even, odd)


def product_kernel(received_ref, w_gate_ref, w_up_ref, w_down_ref, own_ref, send_ref, held):
    rows_x, rows_dy = take_rows(received_ref, held)
    parity = jnp.bitwise_and(lax.axis_index("dp"), 1)
    for half, both in enumerate(products(rows_x, rows_dy, w_gate_ref[...], w_up_ref[...], w_down_ref[...])):
        own, other = split_rows(both, parity)
        own_ref[half] = own
        send_ref[half] = other.astype(BF16)


def pair_kernel(own_ref, taken_ref, out_ref, left_ref):
    dp = lax.axis_index("dp")
    from_partner = 1 - jnp.bitwise_and(dp, 1)
    total = own_ref[...] + taken_ref[from_partner].astype(F32)
    out_ref[...] = total.astype(BF16)
    mine = lax.shift_right_logical(dp, 1)
    kept = own_ref[mine] + taken_ref[from_partner, mine].astype(F32)
    left_ref[...] = kept - kept.astype(BF16).astype(F32)


def activate_body(parts, left):
    total = [parts[i].astype(F32) for i in range(8)]
    while len(total) > 1:
        total = [total[i] + total[i + 1] for i in range(0, len(total), 2)]
    total = total[0] + left
    pre_gate, pre_up, hidden_grad = total[:, :HALF], total[:, HALF : 2 * HALF], total[:, 2 * HALF :]
    sigmoid_gate = jax.nn.sigmoid(pre_gate)
    silu_gate = pre_gate * sigmoid_gate
    hidden = silu_gate * pre_up
    up_grad = hidden_grad * silu_gate
    gate_grad = hidden_grad * pre_up * sigmoid_gate * (1.0 + pre_gate * (1.0 - sigmoid_gate))
    return jnp.concatenate([gate_grad, up_grad, hidden], axis=1).astype(BF16)


def activate_kernel(parts_ref, left_ref, out_ref):
    out_ref[...] = activate_body(parts_ref[...], left_ref[...])


def row_grad_body(packed, w_gate, w_up):
    total = jnp.zeros((ROWS, WIDTH), F32)
    for half in range(2):
        cut = slice(half * HALF, (half + 1) * HALF)
        total += dot(packed[half][:, :HALF], w_gate[:, cut], ((1,), (1,)))
        total += dot(packed[half][:, HALF : 2 * HALF], w_up[:, cut], ((1,), (1,)))
    return total


def row_grad_kernel(packed_ref, w_gate_ref, w_up_ref, out_ref, held):
    total = row_grad_body(packed_ref[...], w_gate_ref[...], w_up_ref[...])
    for place in range(8):
        slot, half = divmod(place, 2)
        if slot < CAP:
            value = total[EXPERTS * slot : EXPERTS * (slot + 1), 128 * half : 128 * (half + 1)]
        else:
            value = jnp.zeros((EXPERTS, 128), F32)
        held[pl.Slice(place, EXPERTS, 8), :] = value
    out_ref[...] = held[...].astype(BF16)


def weight_kernel(packed_ref, received_ref, gate_ref, up_ref, down_ref, held):
    rows_x, rows_dy = take_rows(received_ref, held)
    for half in range(2):
        cut = slice(half * HALF, (half + 1) * HALF)
        gate_ref[:, cut] = dot(rows_x, packed_ref[half, :, :HALF], ((0,), (0,))).astype(BF16)
        up_ref[:, cut] = dot(rows_x, packed_ref[half, :, HALF : 2 * HALF], ((0,), (0,))).astype(BF16)
        down_ref[cut, :] = dot(packed_ref[half, :, 2 * HALF :], rows_dy, ((0,), (0,))).astype(BF16)


def combine_body(back, returned):
    left = dot(back[:TOK], returned, ((1,), (0,)))
    right = dot(back[TOK:], returned, ((1,), (0,)))
    return jnp.concatenate([left, right], axis=1).astype(BF16)


def combine_kernel(back_ref, returned_ref, out_ref):
    out_ref[...] = combine_body(back_ref[...], returned_ref[...])


def call(kernel, outs, flops, *operands, **options):
    shapes = [jax.ShapeDtypeStruct(shape, dtype) for shape, dtype in outs]
    moved = sum(x.size * x.dtype.itemsize for x in [*operands, *shapes])
    return pl.pallas_call(
        kernel,
        out_shape=shapes if len(shapes) > 1 else shapes[0],
        cost_estimate=pl.CostEstimate(flops=flops, bytes_accessed=moved, transcendentals=0),
        compiler_params=pltpu.CompilerParams(vmem_limit_bytes=VMEM_LIMIT),
        **options,
    )(*operands)


HBM = pl.BlockSpec(memory_space=pltpu.HBM)
TAKEN = pltpu.VMEM((2, SLOTS, 128), F32)


def on_device(acts, grad_out, routes, combine, w_gate, w_up, w_down):
    gate_w, up_w, down_w = w_gate[0], w_up[0], w_down[0]
    matmul = 2 * ROWS * WIDTH * HIDDEN

    own, other, back = call(
        dispatch_kernel,
        [((SLOTS // 2, WIDTH), BF16), ((SLOTS // 2, WIDTH), BF16), ((2 * TOK, SLOTS), BF16)],
        4 * matmul,
        *(pltpu.with_memory_space_constraint(x, pltpu.HBM) for x in (routes.T, combine.T, acts, grad_out)),
        in_specs=[HBM] * 4,
        scratch_shapes=[
            pltpu.VMEM((PICKS, TOK), jnp.int32),
            pltpu.VMEM((PICKS, TOK), F32),
            pltpu.VMEM((TOK, WIDTH), BF16),
            pltpu.VMEM((TOK, WIDTH), BF16),
            pltpu.SemaphoreType.DMA((4,)),
        ],
    )
    taken = lax.all_gather(other, "expert", axis=0, axis_index_groups=CORES)
    sent = call(join_kernel, [((SLOTS, WIDTH), BF16)], SLOTS * WIDTH, own, taken)
    received = lax.all_to_all(
        sent.reshape(EXPERTS // 2, 16, WIDTH), "expert", 0, 0, tiled=True, axis_index_groups=SAME_CORE
    ).reshape(SLOTS, WIDTH)

    own, send = call(
        product_kernel,
        [((2, ROWS // 2, PACK), F32), ((2, ROWS // 2, PACK), BF16)],
        3 * matmul,
        received,
        gate_w,
        up_w,
        down_w,
        scratch_shapes=[TAKEN],
    )
    taken = lax.all_gather(send, ("dp", "expert"), axis=0, axis_index_groups=PAIRS)
    eighths = (DP // 2, CHUNK, PACK)
    parts, left = call(
        pair_kernel,
        [(eighths, BF16), ((CHUNK, PACK), F32)],
        ROWS * PACK,
        own.reshape(eighths),
        taken.reshape((2, *eighths)),
    )
    parts = lax.all_to_all(parts, "dp", 0, 0, tiled=True, axis_index_groups=SAME_PARITY)
    block = call(activate_kernel, [((CHUNK, PACK), BF16)], 20 * CHUNK * PACK, parts, left)
    packed = lax.all_gather(block, "dp", axis=0).reshape(2, ROWS, PACK)

    row_grads = call(row_grad_kernel, [((SLOTS, 128), BF16)], 2 * matmul, packed, gate_w, up_w, scratch_shapes=[pltpu.VMEM((SLOTS, 128), F32)])
    returned = lax.all_to_all(row_grads.reshape(EXPERTS, 8, 128), "expert", 0, 0, tiled=True)
    new_gate, new_up, new_down = call(
        weight_kernel,
        [((WIDTH, HIDDEN), BF16), ((WIDTH, HIDDEN), BF16), ((HIDDEN, WIDTH), BF16)],
        3 * matmul,
        packed,
        received,
        scratch_shapes=[TAKEN],
    )
    grad_acts = call(
        combine_kernel, [((TOK, WIDTH), BF16)], 4 * TOK * SLOTS * 128, back, returned.reshape(SLOTS, 128)
    )
    return grad_acts, new_gate[None], new_up[None], new_down[None]


def solution(mesh):
    return jax.shard_map(
        on_device,
        mesh=mesh,
        in_specs=(
            P("expert", "dp"),
            P("expert", "dp"),
            P("expert", None),
            P("expert", None),
            P("expert", "dp", None),
            P("expert", "dp", None),
            P("expert", None, "dp"),
        ),
        out_specs=(
            P("expert", "dp"),
            P("expert", "dp", None),
            P("expert", "dp", None),
            P("expert", None, "dp"),
        ),
        check_vma=False,
    )
```

```python
import functools

import jax
import jax.numpy as jnp
from jax import lax
from jax.experimental import pallas as pl
from jax.experimental.pallas import tpu as pltpu
from jax.sharding import PartitionSpec as P

BF16 = jnp.bfloat16
F32 = jnp.float32
TOK = 16
PICKS = 8
EXPERTS = 64
CAP = 3
ROWS = EXPERTS * CAP
WIDTH = 256
HIDDEN = 768
HALF = HIDDEN // 2
PACK = 3 * HALF
CHUNK = 24
DP = 16
SLOTS = EXPERTS * 8
SAME_PARITY = [[2 * a + b for a in range(DP // 2)] for b in range(2)]

def partner(dp, expert):
    if expert % 2 == 0:
        return dp ^ 1
    return (dp + 1) % DP if dp % 2 else (dp - 1) % DP


PAIRS = [
    [dp * EXPERTS + expert, partner(dp, expert) * EXPERTS + expert]
    for expert in range(EXPERTS)
    for dp in range(0, DP, 2)
]
VMEM_LIMIT = 24 * 1024 * 1024


def dot(a, b, contract):
    return lax.dot_general(a, b, (contract, ((), ())), preferred_element_type=F32)


def iota(shape, dim):
    return lax.broadcasted_iota(jnp.int32, shape, dim)


def column(row):
    diagonal = iota((TOK, TOK), 0) == iota((TOK, TOK), 1)
    spread = jnp.where(diagonal, jnp.broadcast_to(row, (TOK, TOK)), jnp.zeros((), row.dtype))
    return jnp.sum(spread, axis=1, keepdims=True)


def slots_of(routes_t):
    expert = lax.shift_right_logical(iota((TOK, SLOTS), 1), 3)
    hits = [column(routes_t[k : k + 1, :]) == expert for k in range(PICKS)]
    named = functools.reduce(jnp.logical_or, hits)
    earlier = (iota((TOK, TOK), 0) > iota((TOK, TOK), 1)).astype(F32).astype(BF16)
    rank = dot(earlier, named.astype(F32).astype(BF16), ((1,), (0,))).astype(jnp.int32)
    return hits, named, rank


def as_bf16(mask):
    return mask.astype(F32).astype(BF16)


def dispatch_body(routes_t, combine_t, acts, grad_out):
    hits, named, rank = slots_of(routes_t)
    place = jnp.bitwise_and(iota((TOK, SLOTS), 1), 7)
    wanted_x = place == rank
    wanted_dy = place == rank + 4
    choose = [as_bf16(named & wanted_x)] + [as_bf16(hit & wanted_dy) for hit in hits]
    wide = grad_out.astype(F32)
    values = [acts] + [(column(combine_t[k : k + 1, :]) * wide).astype(BF16) for k in range(PICKS)]
    sent = dot(jnp.concatenate(choose, axis=0), jnp.concatenate(values, axis=0), ((0,), (0,)))
    back = [as_bf16(named & (place == 2 * rank + half)) for half in range(2)]
    return sent.astype(BF16), jnp.concatenate(back, axis=0)


def dispatch_kernel(routes, combine, acts, grad_out, sent_ref, back_ref, *scratch):
    held, arrived = scratch[:4], scratch[4]
    copies = [
        pltpu.make_async_copy(source, place, arrived.at[i])
        for i, (source, place) in enumerate(zip((routes, combine, acts, grad_out), held))
    ]
    for copy in copies:
        copy.start()
    for copy in copies:
        copy.wait()
    sent_ref[...], back_ref[...] = dispatch_body(*(place[...] for place in held))


def take_rows(received_ref, held):
    parts = []
    for half in range(2):
        held[half] = received_ref[:, 128 * half : 128 * (half + 1)].astype(F32)
        parts.append([held[half, pl.Slice(place, EXPERTS, 8), :] for place in range(7)])
    full = [jnp.concatenate(pair, axis=1).astype(BF16) for pair in zip(*parts)]
    return jnp.concatenate(full[:CAP], axis=0), jnp.concatenate(full[4 : 4 + CAP], axis=0)


def products(rows_x, rows_dy, w_gate, w_up, w_down):
    gate = dot(rows_x, w_gate, ((1,), (0,)))
    up = dot(rows_x, w_up, ((1,), (0,)))
    back = dot(rows_dy, w_down, ((1,), (1,)))
    cuts = [slice(half * HALF, (half + 1) * HALF) for half in range(2)]
    return [jnp.concatenate([gate[:, cut], up[:, cut], back[:, cut]], axis=1) for cut in cuts]


def split_rows(both, parity):
    even, odd = (
        jnp.concatenate([both[CHUNK * i : CHUNK * (i + 1)] for i in range(first, 8, 2)], axis=0)
        for first in range(2)
    )
    is_odd = parity == 1
    return jnp.where(is_odd, odd, even), jnp.where(is_odd, even, odd)


def product_kernel(received_ref, w_gate_ref, w_up_ref, w_down_ref, own_ref, send_ref, held):
    rows_x, rows_dy = take_rows(received_ref, held)
    parity = jnp.bitwise_and(lax.axis_index("dp"), 1)
    for half, both in enumerate(products(rows_x, rows_dy, w_gate_ref[...], w_up_ref[...], w_down_ref[...])):
        own, other = split_rows(both, parity)
        own_ref[half] = own
        send_ref[half] = other.astype(BF16)


def pair_kernel(own_ref, taken_ref, out_ref, left_ref):
    dp = lax.axis_index("dp")
    from_partner = 1 - jnp.bitwise_and(dp, 1)
    total = own_ref[...] + taken_ref[from_partner].astype(F32)
    out_ref[...] = total.astype(BF16)
    mine = lax.shift_right_logical(dp, 1)
    kept = own_ref[mine] + taken_ref[from_partner, mine].astype(F32)
    left_ref[...] = kept - kept.astype(BF16).astype(F32)


def activate_body(parts, left):
    total = [parts[i].astype(F32) for i in range(8)]
    while len(total) > 1:
        total = [total[i] + total[i + 1] for i in range(0, len(total), 2)]
    total = total[0] + left
    pre_gate, pre_up, hidden_grad = total[:, :HALF], total[:, HALF : 2 * HALF], total[:, 2 * HALF :]
    sigmoid_gate = jax.nn.sigmoid(pre_gate)
    silu_gate = pre_gate * sigmoid_gate
    hidden = silu_gate * pre_up
    up_grad = hidden_grad * silu_gate
    gate_grad = hidden_grad * pre_up * sigmoid_gate * (1.0 + pre_gate * (1.0 - sigmoid_gate))
    return jnp.concatenate([gate_grad, up_grad, hidden], axis=1).astype(BF16)


def activate_kernel(parts_ref, left_ref, out_ref):
    out_ref[...] = activate_body(parts_ref[...], left_ref[...])


def row_grad_body(packed, w_gate, w_up):
    total = jnp.zeros((ROWS, WIDTH), F32)
    for half in range(2):
        cut = slice(half * HALF, (half + 1) * HALF)
        total += dot(packed[half][:, :HALF], w_gate[:, cut], ((1,), (1,)))
        total += dot(packed[half][:, HALF : 2 * HALF], w_up[:, cut], ((1,), (1,)))
    return total


def row_grad_kernel(packed_ref, w_gate_ref, w_up_ref, out_ref, held):
    total = row_grad_body(packed_ref[...], w_gate_ref[...], w_up_ref[...])
    for place in range(8):
        slot, half = divmod(place, 2)
        if slot < CAP:
            value = total[EXPERTS * slot : EXPERTS * (slot + 1), 128 * half : 128 * (half + 1)]
        else:
            value = jnp.zeros((EXPERTS, 128), F32)
        held[pl.Slice(place, EXPERTS, 8), :] = value
    out_ref[...] = held[...].astype(BF16)


def weight_kernel(packed_ref, received_ref, gate_ref, up_ref, down_ref, held):
    rows_x, rows_dy = take_rows(received_ref, held)
    for half in range(2):
        cut = slice(half * HALF, (half + 1) * HALF)
        gate_ref[:, cut] = dot(rows_x, packed_ref[half, :, :HALF], ((0,), (0,))).astype(BF16)
        up_ref[:, cut] = dot(rows_x, packed_ref[half, :, HALF : 2 * HALF], ((0,), (0,))).astype(BF16)
        down_ref[cut, :] = dot(packed_ref[half, :, 2 * HALF :], rows_dy, ((0,), (0,))).astype(BF16)


def combine_body(back, returned):
    left = dot(back[:TOK], returned, ((1,), (0,)))
    right = dot(back[TOK:], returned, ((1,), (0,)))
    return jnp.concatenate([left, right], axis=1).astype(BF16)


def combine_kernel(back_ref, returned_ref, out_ref):
    out_ref[...] = combine_body(back_ref[...], returned_ref[...])


def call(kernel, outs, flops, *operands, **options):
    shapes = [jax.ShapeDtypeStruct(shape, dtype) for shape, dtype in outs]
    moved = sum(x.size * x.dtype.itemsize for x in [*operands, *shapes])
    return pl.pallas_call(
        kernel,
        out_shape=shapes if len(shapes) > 1 else shapes[0],
        cost_estimate=pl.CostEstimate(flops=flops, bytes_accessed=moved, transcendentals=0),
        compiler_params=pltpu.CompilerParams(vmem_limit_bytes=VMEM_LIMIT),
        **options,
    )(*operands)


HBM = pl.BlockSpec(memory_space=pltpu.HBM)
TAKEN = pltpu.VMEM((2, SLOTS, 128), F32)


def on_device(acts, grad_out, routes, combine, w_gate, w_up, w_down):
    gate_w, up_w, down_w = w_gate[0], w_up[0], w_down[0]
    matmul = 2 * ROWS * WIDTH * HIDDEN

    sent, back = call(
        dispatch_kernel,
        [((SLOTS, WIDTH), BF16), ((2 * TOK, SLOTS), BF16)],
        4 * matmul,
        *(pltpu.with_memory_space_constraint(x, pltpu.HBM) for x in (routes.T, combine.T, acts, grad_out)),
        in_specs=[HBM] * 4,
        scratch_shapes=[
            pltpu.VMEM((PICKS, TOK), jnp.int32),
            pltpu.VMEM((PICKS, TOK), F32),
            pltpu.VMEM((TOK, WIDTH), BF16),
            pltpu.VMEM((TOK, WIDTH), BF16),
            pltpu.SemaphoreType.DMA((4,)),
        ],
    )
    received = lax.all_to_all(sent.reshape(EXPERTS, 8, WIDTH), "expert", 0, 0, tiled=True)
    received = received.reshape(SLOTS, WIDTH)

    own, send = call(
        product_kernel,
        [((2, ROWS // 2, PACK), F32), ((2, ROWS // 2, PACK), BF16)],
        3 * matmul,
        received,
        gate_w,
        up_w,
        down_w,
        scratch_shapes=[TAKEN],
    )
    taken = lax.all_gather(send, ("dp", "expert"), axis=0, axis_index_groups=PAIRS)
    eighths = (DP // 2, CHUNK, PACK)
    parts, left = call(
        pair_kernel,
        [(eighths, BF16), ((CHUNK, PACK), F32)],
        ROWS * PACK,
        own.reshape(eighths),
        taken.reshape((2, *eighths)),
    )
    parts = lax.all_to_all(parts, "dp", 0, 0, tiled=True, axis_index_groups=SAME_PARITY)
    block = call(activate_kernel, [((CHUNK, PACK), BF16)], 20 * CHUNK * PACK, parts, left)
    packed = lax.all_gather(block, "dp", axis=0).reshape(2, ROWS, PACK)

    row_grads = call(row_grad_kernel, [((SLOTS, 128), BF16)], 2 * matmul, packed, gate_w, up_w, scratch_shapes=[pltpu.VMEM((SLOTS, 128), F32)])
    returned = lax.all_to_all(row_grads.reshape(EXPERTS, 8, 128), "expert", 0, 0, tiled=True)
    new_gate, new_up, new_down = call(
        weight_kernel,
        [((WIDTH, HIDDEN), BF16), ((WIDTH, HIDDEN), BF16), ((HIDDEN, WIDTH), BF16)],
        3 * matmul,
        packed,
        received,
        scratch_shapes=[TAKEN],
    )
    grad_acts = call(
        combine_kernel, [((TOK, WIDTH), BF16)], 4 * TOK * SLOTS * 128, back, returned.reshape(SLOTS, 128)
    )
    return grad_acts, new_gate[None], new_up[None], new_down[None]


def solution(mesh):
    return jax.shard_map(
        on_device,
        mesh=mesh,
        in_specs=(
            P("expert", "dp"),
            P("expert", "dp"),
            P("expert", None),
            P("expert", None),
            P("expert", "dp", None),
            P("expert", "dp", None),
            P("expert", None, "dp"),
        ),
        out_specs=(
            P("expert", "dp"),
            P("expert", "dp", None),
            P("expert", "dp", None),
            P("expert", None, "dp"),
        ),
        check_vma=False,
    )
```

```python
import functools

import jax
import jax.numpy as jnp
from jax import lax
from jax.experimental import pallas as pl
from jax.experimental.pallas import tpu as pltpu
from jax.sharding import PartitionSpec as P

BF16 = jnp.bfloat16
F32 = jnp.float32
TOK = 16
PICKS = 8
EXPERTS = 64
CAP = 3
ROWS = EXPERTS * CAP
WIDTH = 256
HIDDEN = 768
HALF = HIDDEN // 2
PACK = 3 * HALF
CHUNK = 24
DP = 16
SLOTS = EXPERTS * 8
SAME_PARITY = [[2 * a + b for a in range(DP // 2)] for b in range(2)]

def partner(dp, expert):
    if expert % 2 == 0:
        return dp ^ 1
    return (dp + 1) % DP if dp % 2 else (dp - 1) % DP


PAIRS = [
    [dp * EXPERTS + expert, partner(dp, expert) * EXPERTS + expert]
    for expert in range(EXPERTS)
    for dp in range(0, DP, 2)
]
VMEM_LIMIT = 24 * 1024 * 1024


def dot(a, b, contract):
    return lax.dot_general(a, b, (contract, ((), ())), preferred_element_type=F32)


def iota(shape, dim):
    return lax.broadcasted_iota(jnp.int32, shape, dim)


def column(row):
    diagonal = iota((TOK, TOK), 0) == iota((TOK, TOK), 1)
    spread = jnp.where(diagonal, jnp.broadcast_to(row, (TOK, TOK)), jnp.zeros((), row.dtype))
    return jnp.sum(spread, axis=1, keepdims=True)


def slots_of(routes_t):
    expert = lax.shift_right_logical(iota((TOK, SLOTS), 1), 3)
    hits = [column(routes_t[k : k + 1, :]) == expert for k in range(PICKS)]
    named = functools.reduce(jnp.logical_or, hits)
    earlier = (iota((TOK, TOK), 0) > iota((TOK, TOK), 1)).astype(F32).astype(BF16)
    rank = dot(earlier, named.astype(F32).astype(BF16), ((1,), (0,))).astype(jnp.int32)
    return hits, named, rank


def as_bf16(mask):
    return mask.astype(F32).astype(BF16)


def dispatch_body(routes_t, combine_t, acts, grad_out):
    hits, named, rank = slots_of(routes_t)
    place = jnp.bitwise_and(iota((TOK, SLOTS), 1), 7)
    wanted_x = place == rank
    wanted_dy = place == rank + 4
    choose = [as_bf16(named & wanted_x)] + [as_bf16(hit & wanted_dy) for hit in hits]
    wide = grad_out.astype(F32)
    values = [acts] + [(column(combine_t[k : k + 1, :]) * wide).astype(BF16) for k in range(PICKS)]
    sent = dot(jnp.concatenate(choose, axis=0), jnp.concatenate(values, axis=0), ((0,), (0,)))
    back = [as_bf16(named & (place == 2 * rank + half)) for half in range(2)]
    return sent.astype(BF16), jnp.concatenate(back, axis=0)


def dispatch_kernel(routes, combine, acts, grad_out, sent_ref, back_ref, *scratch):
    held, arrived = scratch[:4], scratch[4]
    copies = [
        pltpu.make_async_copy(source, place, arrived.at[i])
        for i, (source, place) in enumerate(zip((routes, combine, acts, grad_out), held))
    ]
    for copy in copies:
        copy.start()
    for copy in copies:
        copy.wait()
    sent_ref[...], back_ref[...] = dispatch_body(*(place[...] for place in held))


def take_rows(received_ref, held):
    parts = []
    for half in range(2):
        held[half] = received_ref[:, 128 * half : 128 * (half + 1)].astype(F32)
        parts.append([held[half, pl.Slice(place, EXPERTS, 8), :] for place in range(7)])
    full = [jnp.concatenate(pair, axis=1).astype(BF16) for pair in zip(*parts)]
    return jnp.concatenate(full[:CAP], axis=0), jnp.concatenate(full[4 : 4 + CAP], axis=0)


def products(rows_x, rows_dy, w_gate, w_up, w_down):
    gate = dot(rows_x, w_gate, ((1,), (0,)))
    up = dot(rows_x, w_up, ((1,), (0,)))
    back = dot(rows_dy, w_down, ((1,), (1,)))
    cuts = [slice(half * HALF, (half + 1) * HALF) for half in range(2)]
    return [jnp.concatenate([gate[:, cut], up[:, cut], back[:, cut]], axis=1) for cut in cuts]


def split_rows(both, parity):
    even, odd = (
        jnp.concatenate([both[CHUNK * i : CHUNK * (i + 1)] for i in range(first, 8, 2)], axis=0)
        for first in range(2)
    )
    is_odd = parity == 1
    return jnp.where(is_odd, odd, even), jnp.where(is_odd, even, odd)


def product_kernel(received_ref, w_gate_ref, w_up_ref, w_down_ref, own_ref, send_ref, held):
    rows_x, rows_dy = take_rows(received_ref, held)
    parity = jnp.bitwise_and(lax.axis_index("dp"), 1)
    for half, both in enumerate(products(rows_x, rows_dy, w_gate_ref[...], w_up_ref[...], w_down_ref[...])):
        own, other = split_rows(both, parity)
        own_ref[half] = own
        send_ref[half] = other.astype(BF16)


def pair_kernel(own_ref, taken_ref, out_ref, left_ref):
    dp = lax.axis_index("dp")
    from_partner = 1 - jnp.bitwise_and(dp, 1)
    total = own_ref[...] + taken_ref[from_partner].astype(F32)
    out_ref[...] = total.astype(BF16)
    mine = lax.shift_right_logical(dp, 1)
    kept = own_ref[mine] + taken_ref[from_partner, mine].astype(F32)
    left_ref[...] = kept - kept.astype(BF16).astype(F32)


def activate_body(parts, left):
    total = [parts[i].astype(F32) for i in range(8)]
    while len(total) > 1:
        total = [total[i] + total[i + 1] for i in range(0, len(total), 2)]
    total = total[0] + left
    pre_gate, pre_up, hidden_grad = total[:, :HALF], total[:, HALF : 2 * HALF], total[:, 2 * HALF :]
    sigmoid_gate = jax.nn.sigmoid(pre_gate)
    silu_gate = pre_gate * sigmoid_gate
    hidden = silu_gate * pre_up
    up_grad = hidden_grad * silu_gate
    gate_grad = hidden_grad * pre_up * sigmoid_gate * (1.0 + pre_gate * (1.0 - sigmoid_gate))
    return jnp.concatenate([gate_grad, up_grad, hidden], axis=1).astype(BF16)


def activate_kernel(parts_ref, left_ref, out_ref):
    out_ref[...] = activate_body(parts_ref[...], left_ref[...])


def row_grad_body(packed, w_gate, w_up):
    total = jnp.zeros((ROWS, WIDTH), F32)
    for half in range(2):
        cut = slice(half * HALF, (half + 1) * HALF)
        total += dot(packed[half][:, :HALF], w_gate[:, cut], ((1,), (1,)))
        total += dot(packed[half][:, HALF : 2 * HALF], w_up[:, cut], ((1,), (1,)))
    return total


def row_grad_kernel(packed_ref, w_gate_ref, w_up_ref, out_ref, held):
    total = row_grad_body(packed_ref[...], w_gate_ref[...], w_up_ref[...])
    for place in range(8):
        slot, half = divmod(place, 2)
        if slot < CAP:
            value = total[EXPERTS * slot : EXPERTS * (slot + 1), 128 * half : 128 * (half + 1)]
        else:
            value = jnp.zeros((EXPERTS, 128), F32)
        held[pl.Slice(place, EXPERTS, 8), :] = value
    out_ref[...] = held[...].astype(BF16)


def weight_kernel(packed_ref, received_ref, gate_ref, up_ref, down_ref, held):
    rows_x, rows_dy = take_rows(received_ref, held)
    for half in range(2):
        cut = slice(half * HALF, (half + 1) * HALF)
        gate_ref[:, cut] = dot(rows_x, packed_ref[half, :, :HALF], ((0,), (0,))).astype(BF16)
        up_ref[:, cut] = dot(rows_x, packed_ref[half, :, HALF : 2 * HALF], ((0,), (0,))).astype(BF16)
        down_ref[cut, :] = dot(packed_ref[half, :, 2 * HALF :], rows_dy, ((0,), (0,))).astype(BF16)


def combine_body(back, returned):
    left = dot(back[:TOK], returned, ((1,), (0,)))
    right = dot(back[TOK:], returned, ((1,), (0,)))
    return jnp.concatenate([left, right], axis=1).astype(BF16)


def final_kernel(packed_ref, received_ref, back_ref, returned_ref, acts_ref, gate_ref, up_ref, down_ref, held):
    acts_ref[...] = combine_body(back_ref[...], returned_ref[...])
    weight_kernel(packed_ref, received_ref, gate_ref, up_ref, down_ref, held)


def call(kernel, outs, flops, *operands, **options):
    shapes = [jax.ShapeDtypeStruct(shape, dtype) for shape, dtype in outs]
    moved = sum(x.size * x.dtype.itemsize for x in [*operands, *shapes])
    return pl.pallas_call(
        kernel,
        out_shape=shapes if len(shapes) > 1 else shapes[0],
        cost_estimate=pl.CostEstimate(flops=flops, bytes_accessed=moved, transcendentals=0),
        compiler_params=pltpu.CompilerParams(vmem_limit_bytes=VMEM_LIMIT),
        **options,
    )(*operands)


HBM = pl.BlockSpec(memory_space=pltpu.HBM)
TAKEN = pltpu.VMEM((2, SLOTS, 128), F32)


def on_device(acts, grad_out, routes, combine, w_gate, w_up, w_down):
    gate_w, up_w, down_w = w_gate[0], w_up[0], w_down[0]
    matmul = 2 * ROWS * WIDTH * HIDDEN

    sent, back = call(
        dispatch_kernel,
        [((SLOTS, WIDTH), BF16), ((2 * TOK, SLOTS), BF16)],
        4 * matmul,
        *(pltpu.with_memory_space_constraint(x, pltpu.HBM) for x in (routes.T, combine.T, acts, grad_out)),
        in_specs=[HBM] * 4,
        scratch_shapes=[
            pltpu.VMEM((PICKS, TOK), jnp.int32),
            pltpu.VMEM((PICKS, TOK), F32),
            pltpu.VMEM((TOK, WIDTH), BF16),
            pltpu.VMEM((TOK, WIDTH), BF16),
            pltpu.SemaphoreType.DMA((4,)),
        ],
    )
    received = lax.all_to_all(sent.reshape(EXPERTS, 8, WIDTH), "expert", 0, 0, tiled=True)
    received = received.reshape(SLOTS, WIDTH)

    own, send = call(
        product_kernel,
        [((2, ROWS // 2, PACK), F32), ((2, ROWS // 2, PACK), BF16)],
        3 * matmul,
        received,
        gate_w,
        up_w,
        down_w,
        scratch_shapes=[TAKEN],
    )
    taken = lax.all_gather(send, ("dp", "expert"), axis=0, axis_index_groups=PAIRS)
    eighths = (DP // 2, CHUNK, PACK)
    parts, left = call(
        pair_kernel,
        [(eighths, BF16), ((CHUNK, PACK), F32)],
        ROWS * PACK,
        own.reshape(eighths),
        taken.reshape((2, *eighths)),
    )
    parts = lax.all_to_all(parts, "dp", 0, 0, tiled=True, axis_index_groups=SAME_PARITY)
    block = call(activate_kernel, [((CHUNK, PACK), BF16)], 20 * CHUNK * PACK, parts, left)
    packed = lax.all_gather(block, "dp", axis=0).reshape(2, ROWS, PACK)

    row_grads = call(row_grad_kernel, [((SLOTS, 128), BF16)], 2 * matmul, packed, gate_w, up_w, scratch_shapes=[pltpu.VMEM((SLOTS, 128), F32)])
    returned = lax.all_to_all(row_grads.reshape(EXPERTS, 8, 128), "expert", 0, 0, tiled=True)
    grad_acts, new_gate, new_up, new_down = call(
        final_kernel,
        [((TOK, WIDTH), BF16), ((WIDTH, HIDDEN), BF16), ((WIDTH, HIDDEN), BF16), ((HIDDEN, WIDTH), BF16)],
        3 * matmul,
        packed,
        received,
        back,
        returned.reshape(SLOTS, 128),
        scratch_shapes=[TAKEN],
    )
    return grad_acts, new_gate[None], new_up[None], new_down[None]


def solution(mesh):
    return jax.shard_map(
        on_device,
        mesh=mesh,
        in_specs=(
            P("expert", "dp"),
            P("expert", "dp"),
            P("expert", None),
            P("expert", None),
            P("expert", "dp", None),
            P("expert", "dp", None),
            P("expert", None, "dp"),
        ),
        out_specs=(
            P("expert", "dp"),
            P("expert", "dp", None),
            P("expert", "dp", None),
            P("expert", None, "dp"),
        ),
        check_vma=False,
    )
```

```python
import functools

import jax
import jax.numpy as jnp
from jax import lax
from jax.experimental import pallas as pl
from jax.experimental.pallas import tpu as pltpu
from jax.sharding import PartitionSpec as P

BF16 = jnp.bfloat16
F32 = jnp.float32
TOK = 16
PICKS = 8
EXPERTS = 64
CAP = 3
ROWS = EXPERTS * CAP
WIDTH = 256
HIDDEN = 768
HALF = HIDDEN // 2
PACK = 3 * HALF
CHUNK = 24
DP = 16
SLOTS = EXPERTS * 8
QUARTER = DP // 4
FAR = [[4 * a + low for a in range(QUARTER)] for low in range(4)]


def pairs(distance):
    firsts = [dp for dp in range(DP) if not dp & distance]
    sign = [distance, -distance]
    return [
        [dp * EXPERTS + expert, (dp + sign[expert % 2]) % DP * EXPERTS + expert]
        for expert in range(EXPERTS)
        for dp in firsts
    ]


VMEM_LIMIT = 24 * 1024 * 1024


def dot(a, b, contract):
    return lax.dot_general(a, b, (contract, ((), ())), preferred_element_type=F32)


def iota(shape, dim):
    return lax.broadcasted_iota(jnp.int32, shape, dim)


def column(row):
    diagonal = iota((TOK, TOK), 0) == iota((TOK, TOK), 1)
    spread = jnp.where(diagonal, jnp.broadcast_to(row, (TOK, TOK)), jnp.zeros((), row.dtype))
    return jnp.sum(spread, axis=1, keepdims=True)


def slots_of(routes_t):
    expert = lax.shift_right_logical(iota((TOK, SLOTS), 1), 3)
    hits = [column(routes_t[k : k + 1, :]) == expert for k in range(PICKS)]
    named = functools.reduce(jnp.logical_or, hits)
    earlier = (iota((TOK, TOK), 0) > iota((TOK, TOK), 1)).astype(F32).astype(BF16)
    rank = dot(earlier, named.astype(F32).astype(BF16), ((1,), (0,))).astype(jnp.int32)
    return hits, named, rank


def as_bf16(mask):
    return mask.astype(F32).astype(BF16)


def dispatch_body(routes_t, combine_t, acts, grad_out):
    hits, named, rank = slots_of(routes_t)
    place = jnp.bitwise_and(iota((TOK, SLOTS), 1), 7)
    wanted_x = place == rank
    wanted_dy = place == rank + 4
    choose = [as_bf16(named & wanted_x)] + [as_bf16(hit & wanted_dy) for hit in hits]
    wide = grad_out.astype(F32)
    values = [acts] + [(column(combine_t[k : k + 1, :]) * wide).astype(BF16) for k in range(PICKS)]
    sent = dot(jnp.concatenate(choose, axis=0), jnp.concatenate(values, axis=0), ((0,), (0,)))
    back = [as_bf16(named & (place == 2 * rank + half)) for half in range(2)]
    return sent.astype(BF16), jnp.concatenate(back, axis=0)


def dispatch_kernel(routes, combine, acts, grad_out, sent_ref, back_ref, *scratch):
    held, arrived = scratch[:4], scratch[4]
    copies = [
        pltpu.make_async_copy(source, place, arrived.at[i])
        for i, (source, place) in enumerate(zip((routes, combine, acts, grad_out), held))
    ]
    for copy in copies:
        copy.start()
    for copy in copies:
        copy.wait()
    sent_ref[...], back_ref[...] = dispatch_body(*(place[...] for place in held))


def take_rows(received_ref, held):
    parts = []
    for half in range(2):
        held[half] = received_ref[:, 128 * half : 128 * (half + 1)].astype(F32)
        parts.append([held[half, pl.Slice(place, EXPERTS, 8), :] for place in range(7)])
    full = [jnp.concatenate(pair, axis=1).astype(BF16) for pair in zip(*parts)]
    return jnp.concatenate(full[:CAP], axis=0), jnp.concatenate(full[4 : 4 + CAP], axis=0)


def products(rows_x, rows_dy, w_gate, w_up, w_down):
    gate = dot(rows_x, w_gate, ((1,), (0,)))
    up = dot(rows_x, w_up, ((1,), (0,)))
    back = dot(rows_dy, w_down, ((1,), (1,)))
    cuts = [slice(half * HALF, (half + 1) * HALF) for half in range(2)]
    return [jnp.concatenate([gate[:, cut], up[:, cut], back[:, cut]], axis=1) for cut in cuts]


def split_rows(both, parity):
    even, odd = (
        jnp.concatenate([both[CHUNK * i : CHUNK * (i + 1)] for i in range(first, 8, 2)], axis=0)
        for first in range(2)
    )
    is_odd = parity == 1
    return jnp.where(is_odd, odd, even), jnp.where(is_odd, even, odd)


def product_kernel(received_ref, w_gate_ref, w_up_ref, w_down_ref, own_ref, send_ref, held):
    rows_x, rows_dy = take_rows(received_ref, held)
    parity = jnp.bitwise_and(lax.axis_index("dp"), 1)
    for half, both in enumerate(products(rows_x, rows_dy, w_gate_ref[...], w_up_ref[...], w_down_ref[...])):
        own, other = split_rows(both, parity)
        own_ref[half] = own
        send_ref[half] = other.astype(BF16)


def first_kernel(own_ref, taken_ref, keep_ref, send_ref):
    dp = lax.axis_index("dp")
    from_partner = 1 - jnp.bitwise_and(dp, 1)
    mine = jnp.bitwise_and(lax.shift_right_logical(dp, 1), 1)
    for i in range(QUARTER):
        keep_ref[i] = own_ref[i, mine] + taken_ref[from_partner, i, mine].astype(F32)
        send_ref[i] = (own_ref[i, 1 - mine] + taken_ref[from_partner, i, 1 - mine].astype(F32)).astype(BF16)


def second_kernel(own_ref, taken_ref, out_ref):
    from_partner = 1 - jnp.bitwise_and(lax.shift_right_logical(lax.axis_index("dp"), 1), 1)
    out_ref[...] = own_ref[...] + taken_ref[from_partner].astype(F32)


def activate_body(parts):
    total = [parts[i] for i in range(QUARTER)]
    while len(total) > 1:
        total = [total[i] + total[i + 1] for i in range(0, len(total), 2)]
    total = total[0]
    pre_gate, pre_up, hidden_grad = total[:, :HALF], total[:, HALF : 2 * HALF], total[:, 2 * HALF :]
    sigmoid_gate = jax.nn.sigmoid(pre_gate)
    silu_gate = pre_gate * sigmoid_gate
    hidden = silu_gate * pre_up
    up_grad = hidden_grad * silu_gate
    gate_grad = hidden_grad * pre_up * sigmoid_gate * (1.0 + pre_gate * (1.0 - sigmoid_gate))
    return jnp.concatenate([gate_grad, up_grad, hidden], axis=1).astype(BF16)


def activate_kernel(parts_ref, out_ref):
    out_ref[...] = activate_body(parts_ref[...])


def row_grad_body(packed, w_gate, w_up):
    total = jnp.zeros((ROWS, WIDTH), F32)
    for half in range(2):
        cut = slice(half * HALF, (half + 1) * HALF)
        total += dot(packed[half][:, :HALF], w_gate[:, cut], ((1,), (1,)))
        total += dot(packed[half][:, HALF : 2 * HALF], w_up[:, cut], ((1,), (1,)))
    return total


def row_grad_kernel(packed_ref, w_gate_ref, w_up_ref, out_ref, held):
    total = row_grad_body(packed_ref[...], w_gate_ref[...], w_up_ref[...])
    for place in range(8):
        slot, half = divmod(place, 2)
        if slot < CAP:
            value = total[EXPERTS * slot : EXPERTS * (slot + 1), 128 * half : 128 * (half + 1)]
        else:
            value = jnp.zeros((EXPERTS, 128), F32)
        held[pl.Slice(place, EXPERTS, 8), :] = value
    out_ref[...] = held[...].astype(BF16)


def weight_kernel(packed_ref, received_ref, gate_ref, up_ref, down_ref, held):
    rows_x, rows_dy = take_rows(received_ref, held)
    for half in range(2):
        cut = slice(half * HALF, (half + 1) * HALF)
        gate_ref[:, cut] = dot(rows_x, packed_ref[half, :, :HALF], ((0,), (0,))).astype(BF16)
        up_ref[:, cut] = dot(rows_x, packed_ref[half, :, HALF : 2 * HALF], ((0,), (0,))).astype(BF16)
        down_ref[cut, :] = dot(packed_ref[half, :, 2 * HALF :], rows_dy, ((0,), (0,))).astype(BF16)


def combine_body(back, returned):
    left = dot(back[:TOK], returned, ((1,), (0,)))
    right = dot(back[TOK:], returned, ((1,), (0,)))
    return jnp.concatenate([left, right], axis=1).astype(BF16)


def final_kernel(packed_ref, received_ref, back_ref, returned_ref, acts_ref, gate_ref, up_ref, down_ref, held):
    acts_ref[...] = combine_body(back_ref[...], returned_ref[...])
    weight_kernel(packed_ref, received_ref, gate_ref, up_ref, down_ref, held)


def call(kernel, outs, flops, *operands, **options):
    shapes = [jax.ShapeDtypeStruct(shape, dtype) for shape, dtype in outs]
    moved = sum(x.size * x.dtype.itemsize for x in [*operands, *shapes])
    return pl.pallas_call(
        kernel,
        out_shape=shapes if len(shapes) > 1 else shapes[0],
        cost_estimate=pl.CostEstimate(flops=flops, bytes_accessed=moved, transcendentals=0),
        compiler_params=pltpu.CompilerParams(vmem_limit_bytes=VMEM_LIMIT),
        **options,
    )(*operands)


HBM = pl.BlockSpec(memory_space=pltpu.HBM)
TAKEN = pltpu.VMEM((2, SLOTS, 128), F32)


def on_device(acts, grad_out, routes, combine, w_gate, w_up, w_down):
    gate_w, up_w, down_w = w_gate[0], w_up[0], w_down[0]
    matmul = 2 * ROWS * WIDTH * HIDDEN

    sent, back = call(
        dispatch_kernel,
        [((SLOTS, WIDTH), BF16), ((2 * TOK, SLOTS), BF16)],
        4 * matmul,
        *(pltpu.with_memory_space_constraint(x, pltpu.HBM) for x in (routes.T, combine.T, acts, grad_out)),
        in_specs=[HBM] * 4,
        scratch_shapes=[
            pltpu.VMEM((PICKS, TOK), jnp.int32),
            pltpu.VMEM((PICKS, TOK), F32),
            pltpu.VMEM((TOK, WIDTH), BF16),
            pltpu.VMEM((TOK, WIDTH), BF16),
            pltpu.SemaphoreType.DMA((4,)),
        ],
    )
    received = lax.all_to_all(sent.reshape(EXPERTS, 8, WIDTH), "expert", 0, 0, tiled=True)
    received = received.reshape(SLOTS, WIDTH)

    own, send = call(
        product_kernel,
        [((2, ROWS // 2, PACK), F32), ((2, ROWS // 2, PACK), BF16)],
        3 * matmul,
        received,
        gate_w,
        up_w,
        down_w,
        scratch_shapes=[TAKEN],
    )
    mesh_axes = ("dp", "expert")
    taken = lax.all_gather(send, mesh_axes, axis=0, axis_index_groups=pairs(1))
    eighths, quarters = (QUARTER, 2, CHUNK, PACK), (QUARTER, CHUNK, PACK)
    keep, send = call(
        first_kernel,
        [(quarters, F32), (quarters, BF16)],
        ROWS * PACK,
        own.reshape(eighths),
        taken.reshape((2, *eighths)),
    )
    taken = lax.all_gather(send, mesh_axes, axis=0, axis_index_groups=pairs(2))
    parts = call(second_kernel, [(quarters, F32)], ROWS * PACK // 2, keep, taken)
    parts = lax.all_to_all(parts, "dp", 0, 0, tiled=True, axis_index_groups=FAR)
    block = call(activate_kernel, [((CHUNK, PACK), BF16)], 20 * CHUNK * PACK, parts)
    packed = lax.all_gather(block, "dp", axis=0).reshape(2, ROWS, PACK)

    row_grads = call(row_grad_kernel, [((SLOTS, 128), BF16)], 2 * matmul, packed, gate_w, up_w, scratch_shapes=[pltpu.VMEM((SLOTS, 128), F32)])
    returned = lax.all_to_all(row_grads.reshape(EXPERTS, 8, 128), "expert", 0, 0, tiled=True)
    grad_acts, new_gate, new_up, new_down = call(
        final_kernel,
        [((TOK, WIDTH), BF16), ((WIDTH, HIDDEN), BF16), ((WIDTH, HIDDEN), BF16), ((HIDDEN, WIDTH), BF16)],
        3 * matmul,
        packed,
        received,
        back,
        returned.reshape(SLOTS, 128),
        scratch_shapes=[TAKEN],
    )
    return grad_acts, new_gate[None], new_up[None], new_down[None]


def solution(mesh):
    return jax.shard_map(
        on_device,
        mesh=mesh,
        in_specs=(
            P("expert", "dp"),
            P("expert", "dp"),
            P("expert", None),
            P("expert", None),
            P("expert", "dp", None),
            P("expert", "dp", None),
            P("expert", None, "dp"),
        ),
        out_specs=(
            P("expert", "dp"),
            P("expert", "dp", None),
            P("expert", "dp", None),
            P("expert", None, "dp"),
        ),
        check_vma=False,
    )
```

```python
import functools

import jax
import jax.numpy as jnp
from jax import lax
from jax.experimental import pallas as pl
from jax.experimental.pallas import tpu as pltpu
from jax.sharding import PartitionSpec as P

BF16 = jnp.bfloat16
F32 = jnp.float32
TOK = 16
PICKS = 8
EXPERTS = 64
CAP = 3
ROWS = EXPERTS * CAP
WIDTH = 256
HIDDEN = 768
HALF = HIDDEN // 2
PACK = 3 * HALF
CHUNK = 24
DP = 16
SLOTS = EXPERTS * 8
QUARTER = DP // 4
FAR = [[4 * a + low for a in range(QUARTER)] for low in range(4)]


def pairs(distance):
    firsts = [dp for dp in range(DP) if not dp & distance]
    sign = [distance, -distance]
    return [
        [dp * EXPERTS + expert, (dp + sign[expert % 2]) % DP * EXPERTS + expert]
        for expert in range(EXPERTS)
        for dp in firsts
    ]


VMEM_LIMIT = 24 * 1024 * 1024


def dot(a, b, contract):
    return lax.dot_general(a, b, (contract, ((), ())), preferred_element_type=F32)


def iota(shape, dim):
    return lax.broadcasted_iota(jnp.int32, shape, dim)


def column(row):
    diagonal = iota((TOK, TOK), 0) == iota((TOK, TOK), 1)
    spread = jnp.where(diagonal, jnp.broadcast_to(row, (TOK, TOK)), jnp.zeros((), row.dtype))
    return jnp.sum(spread, axis=1, keepdims=True)


def slots_of(routes_t):
    expert = lax.shift_right_logical(iota((TOK, SLOTS), 1), 3)
    hits = [column(routes_t[k : k + 1, :]) == expert for k in range(PICKS)]
    named = functools.reduce(jnp.logical_or, hits)
    earlier = (iota((TOK, TOK), 0) > iota((TOK, TOK), 1)).astype(F32).astype(BF16)
    rank = dot(earlier, named.astype(F32).astype(BF16), ((1,), (0,))).astype(jnp.int32)
    return hits, named, rank


def as_bf16(mask):
    return mask.astype(F32).astype(BF16)


def dispatch_body(routes_t, combine_t, acts, grad_out):
    hits, named, rank = slots_of(routes_t)
    place = jnp.bitwise_and(iota((TOK, SLOTS), 1), 7)
    wanted_x = place == rank
    wanted_dy = place == rank + 4
    choose = [as_bf16(named & wanted_x)] + [as_bf16(hit & wanted_dy) for hit in hits]
    wide = grad_out.astype(F32)
    values = [acts] + [(column(combine_t[k : k + 1, :]) * wide).astype(BF16) for k in range(PICKS)]
    sent = dot(jnp.concatenate(choose, axis=0), jnp.concatenate(values, axis=0), ((0,), (0,)))
    back = [as_bf16(named & (place == 2 * rank + half)) for half in range(2)]
    return sent.astype(BF16), jnp.concatenate(back, axis=0)


def dispatch_kernel(routes, combine, acts, grad_out, sent_ref, back_ref, *scratch):
    held, arrived = scratch[:4], scratch[4]
    copies = [
        pltpu.make_async_copy(source, place, arrived.at[i])
        for i, (source, place) in enumerate(zip((routes, combine, acts, grad_out), held))
    ]
    for copy in copies:
        copy.start()
    for copy in copies:
        copy.wait()
    sent_ref[...], back_ref[...] = dispatch_body(*(place[...] for place in held))


def take_rows(received_ref, held):
    parts = []
    for half in range(2):
        held[half] = received_ref[:, 128 * half : 128 * (half + 1)].astype(F32)
        parts.append([held[half, pl.Slice(place, EXPERTS, 8), :] for place in range(7)])
    full = [jnp.concatenate(pair, axis=1).astype(BF16) for pair in zip(*parts)]
    return jnp.concatenate(full[:CAP], axis=0), jnp.concatenate(full[4 : 4 + CAP], axis=0)


def products(rows_x, rows_dy, w_gate, w_up, w_down):
    gate = dot(rows_x, w_gate, ((1,), (0,)))
    up = dot(rows_x, w_up, ((1,), (0,)))
    back = dot(rows_dy, w_down, ((1,), (1,)))
    cuts = [slice(half * HALF, (half + 1) * HALF) for half in range(2)]
    return [jnp.concatenate([gate[:, cut], up[:, cut], back[:, cut]], axis=1) for cut in cuts]


def split_rows(both, parity):
    even, odd = (
        jnp.concatenate([both[CHUNK * i : CHUNK * (i + 1)] for i in range(first, 8, 2)], axis=0)
        for first in range(2)
    )
    is_odd = parity == 1
    return jnp.where(is_odd, odd, even), jnp.where(is_odd, even, odd)


def product_kernel(received_ref, w_gate_ref, w_up_ref, w_down_ref, own_ref, send_ref, held):
    rows_x, rows_dy = take_rows(received_ref, held)
    parity = jnp.bitwise_and(lax.axis_index("dp"), 1)
    for half, both in enumerate(products(rows_x, rows_dy, w_gate_ref[...], w_up_ref[...], w_down_ref[...])):
        own, other = split_rows(both, parity)
        own_ref[half] = own
        send_ref[half] = other.astype(BF16)


def first_kernel(own_ref, taken_ref, keep_ref, send_ref):
    dp = lax.axis_index("dp")
    from_partner = 1 - jnp.bitwise_and(dp, 1)
    mine = jnp.bitwise_and(lax.shift_right_logical(dp, 1), 1)
    for i in range(QUARTER):
        keep_ref[i] = own_ref[i, mine] + taken_ref[from_partner, i, mine].astype(F32)
        send_ref[i] = (own_ref[i, 1 - mine] + taken_ref[from_partner, i, 1 - mine].astype(F32)).astype(BF16)


def second_kernel(own_ref, taken_ref, out_ref, left_ref):
    dp = lax.axis_index("dp")
    from_partner = 1 - jnp.bitwise_and(lax.shift_right_logical(dp, 1), 1)
    out_ref[...] = (own_ref[...] + taken_ref[from_partner].astype(F32)).astype(BF16)
    mine = lax.shift_right_logical(dp, 2)
    kept = own_ref[mine] + taken_ref[from_partner, mine].astype(F32)
    left_ref[...] = kept - kept.astype(BF16).astype(F32)


def activate_body(parts, left):
    total = [parts[i].astype(F32) for i in range(QUARTER)]
    while len(total) > 1:
        total = [total[i] + total[i + 1] for i in range(0, len(total), 2)]
    total = total[0] + left
    pre_gate, pre_up, hidden_grad = total[:, :HALF], total[:, HALF : 2 * HALF], total[:, 2 * HALF :]
    sigmoid_gate = jax.nn.sigmoid(pre_gate)
    silu_gate = pre_gate * sigmoid_gate
    hidden = silu_gate * pre_up
    up_grad = hidden_grad * silu_gate
    gate_grad = hidden_grad * pre_up * sigmoid_gate * (1.0 + pre_gate * (1.0 - sigmoid_gate))
    return jnp.concatenate([gate_grad, up_grad, hidden], axis=1).astype(BF16)


def activate_kernel(parts_ref, left_ref, out_ref):
    out_ref[...] = activate_body(parts_ref[...], left_ref[...])


def row_grad_body(packed, w_gate, w_up):
    total = jnp.zeros((ROWS, WIDTH), F32)
    for half in range(2):
        cut = slice(half * HALF, (half + 1) * HALF)
        total += dot(packed[half][:, :HALF], w_gate[:, cut], ((1,), (1,)))
        total += dot(packed[half][:, HALF : 2 * HALF], w_up[:, cut], ((1,), (1,)))
    return total


def row_grad_kernel(packed_ref, w_gate_ref, w_up_ref, out_ref, held):
    total = row_grad_body(packed_ref[...], w_gate_ref[...], w_up_ref[...])
    for place in range(8):
        slot, half = divmod(place, 2)
        if slot < CAP:
            value = total[EXPERTS * slot : EXPERTS * (slot + 1), 128 * half : 128 * (half + 1)]
        else:
            value = jnp.zeros((EXPERTS, 128), F32)
        held[pl.Slice(place, EXPERTS, 8), :] = value
    out_ref[...] = held[...].astype(BF16)


def weight_kernel(packed_ref, received_ref, gate_ref, up_ref, down_ref, held):
    rows_x, rows_dy = take_rows(received_ref, held)
    for half in range(2):
        cut = slice(half * HALF, (half + 1) * HALF)
        gate_ref[:, cut] = dot(rows_x, packed_ref[half, :, :HALF], ((0,), (0,))).astype(BF16)
        up_ref[:, cut] = dot(rows_x, packed_ref[half, :, HALF : 2 * HALF], ((0,), (0,))).astype(BF16)
        down_ref[cut, :] = dot(packed_ref[half, :, 2 * HALF :], rows_dy, ((0,), (0,))).astype(BF16)


def combine_body(back, returned):
    left = dot(back[:TOK], returned, ((1,), (0,)))
    right = dot(back[TOK:], returned, ((1,), (0,)))
    return jnp.concatenate([left, right], axis=1).astype(BF16)


def final_kernel(packed_ref, received_ref, back_ref, returned_ref, acts_ref, gate_ref, up_ref, down_ref, held):
    acts_ref[...] = combine_body(back_ref[...], returned_ref[...])
    weight_kernel(packed_ref, received_ref, gate_ref, up_ref, down_ref, held)


def call(kernel, outs, flops, *operands, **options):
    shapes = [jax.ShapeDtypeStruct(shape, dtype) for shape, dtype in outs]
    moved = sum(x.size * x.dtype.itemsize for x in [*operands, *shapes])
    return pl.pallas_call(
        kernel,
        out_shape=shapes if len(shapes) > 1 else shapes[0],
        cost_estimate=pl.CostEstimate(flops=flops, bytes_accessed=moved, transcendentals=0),
        compiler_params=pltpu.CompilerParams(vmem_limit_bytes=VMEM_LIMIT),
        **options,
    )(*operands)


HBM = pl.BlockSpec(memory_space=pltpu.HBM)
TAKEN = pltpu.VMEM((2, SLOTS, 128), F32)


def on_device(acts, grad_out, routes, combine, w_gate, w_up, w_down):
    gate_w, up_w, down_w = w_gate[0], w_up[0], w_down[0]
    matmul = 2 * ROWS * WIDTH * HIDDEN

    sent, back = call(
        dispatch_kernel,
        [((SLOTS, WIDTH), BF16), ((2 * TOK, SLOTS), BF16)],
        4 * matmul,
        *(pltpu.with_memory_space_constraint(x, pltpu.HBM) for x in (routes.T, combine.T, acts, grad_out)),
        in_specs=[HBM] * 4,
        scratch_shapes=[
            pltpu.VMEM((PICKS, TOK), jnp.int32),
            pltpu.VMEM((PICKS, TOK), F32),
            pltpu.VMEM((TOK, WIDTH), BF16),
            pltpu.VMEM((TOK, WIDTH), BF16),
            pltpu.SemaphoreType.DMA((4,)),
        ],
    )
    received = lax.all_to_all(sent.reshape(EXPERTS, 8, WIDTH), "expert", 0, 0, tiled=True)
    received = received.reshape(SLOTS, WIDTH)

    own, send = call(
        product_kernel,
        [((2, ROWS // 2, PACK), F32), ((2, ROWS // 2, PACK), BF16)],
        3 * matmul,
        received,
        gate_w,
        up_w,
        down_w,
        scratch_shapes=[TAKEN],
    )
    mesh_axes = ("dp", "expert")
    taken = lax.all_gather(send, mesh_axes, axis=0, axis_index_groups=pairs(1))
    eighths, quarters = (QUARTER, 2, CHUNK, PACK), (QUARTER, CHUNK, PACK)
    keep, send = call(
        first_kernel,
        [(quarters, F32), (quarters, BF16)],
        ROWS * PACK,
        own.reshape(eighths),
        taken.reshape((2, *eighths)),
    )
    taken = lax.all_gather(send, mesh_axes, axis=0, axis_index_groups=pairs(2))
    parts, left = call(
        second_kernel, [(quarters, BF16), ((CHUNK, PACK), F32)], ROWS * PACK // 2, keep, taken
    )
    parts = lax.all_to_all(parts, "dp", 0, 0, tiled=True, axis_index_groups=FAR)
    block = call(activate_kernel, [((CHUNK, PACK), BF16)], 20 * CHUNK * PACK, parts, left)
    packed = lax.all_gather(block, "dp", axis=0).reshape(2, ROWS, PACK)

    row_grads = call(row_grad_kernel, [((SLOTS, 128), BF16)], 2 * matmul, packed, gate_w, up_w, scratch_shapes=[pltpu.VMEM((SLOTS, 128), F32)])
    returned = lax.all_to_all(row_grads.reshape(EXPERTS, 8, 128), "expert", 0, 0, tiled=True)
    grad_acts, new_gate, new_up, new_down = call(
        final_kernel,
        [((TOK, WIDTH), BF16), ((WIDTH, HIDDEN), BF16), ((WIDTH, HIDDEN), BF16), ((HIDDEN, WIDTH), BF16)],
        3 * matmul,
        packed,
        received,
        back,
        returned.reshape(SLOTS, 128),
        scratch_shapes=[TAKEN],
    )
    return grad_acts, new_gate[None], new_up[None], new_down[None]


def solution(mesh):
    return jax.shard_map(
        on_device,
        mesh=mesh,
        in_specs=(
            P("expert", "dp"),
            P("expert", "dp"),
            P("expert", None),
            P("expert", None),
            P("expert", "dp", None),
            P("expert", "dp", None),
            P("expert", None, "dp"),
        ),
        out_specs=(
            P("expert", "dp"),
            P("expert", "dp", None),
            P("expert", "dp", None),
            P("expert", None, "dp"),
        ),
        check_vma=False,
    )
```

```python
import functools

import jax
import jax.numpy as jnp
from jax import lax
from jax.experimental import pallas as pl
from jax.experimental.pallas import tpu as pltpu
from jax.sharding import PartitionSpec as P

BF16 = jnp.bfloat16
F32 = jnp.float32
TOK = 16
PICKS = 8
EXPERTS = 64
CAP = 3
ROWS = EXPERTS * CAP
WIDTH = 256
HIDDEN = 768
HALF = HIDDEN // 2
PACK = 3 * HALF
CHUNK = 24
DP = 16
SLOTS = EXPERTS * 8
QUARTER = DP // 4
FAR = [[4 * a + low for a in range(QUARTER)] for low in range(4)]


def pairs(distance):
    firsts = [dp for dp in range(DP) if not dp & distance]
    sign = [distance, -distance]
    return [
        [dp * EXPERTS + expert, (dp + sign[expert % 2]) % DP * EXPERTS + expert]
        for expert in range(EXPERTS)
        for dp in firsts
    ]


VMEM_LIMIT = 24 * 1024 * 1024


def dot(a, b, contract):
    return lax.dot_general(a, b, (contract, ((), ())), preferred_element_type=F32)


def iota(shape, dim):
    return lax.broadcasted_iota(jnp.int32, shape, dim)


def column(row):
    diagonal = iota((TOK, TOK), 0) == iota((TOK, TOK), 1)
    spread = jnp.where(diagonal, jnp.broadcast_to(row, (TOK, TOK)), jnp.zeros((), row.dtype))
    return jnp.sum(spread, axis=1, keepdims=True)


def slots_of(routes_t):
    expert = lax.shift_right_logical(iota((TOK, SLOTS), 1), 3)
    hits = [column(routes_t[k : k + 1, :]) == expert for k in range(PICKS)]
    named = functools.reduce(jnp.logical_or, hits)
    counts = named.astype(F32)
    row = iota((TOK, SLOTS), 0)
    running = counts
    for step in (1, 2, 4, 8):
        running += jnp.where(row >= step, jnp.roll(running, step, axis=0), 0.0)
    rank = (running - counts).astype(jnp.int32)
    return hits, named, rank


def as_bf16(mask):
    return mask.astype(F32).astype(BF16)


def dispatch_body(routes_t, combine_t, acts, grad_out):
    hits, named, rank = slots_of(routes_t)
    place = jnp.bitwise_and(iota((TOK, SLOTS), 1), 7)
    wanted_x = place == rank
    wanted_dy = place == rank + 4
    choose = [as_bf16(named & wanted_x)] + [as_bf16(hit & wanted_dy) for hit in hits]
    wide = grad_out.astype(F32)
    values = [acts] + [(column(combine_t[k : k + 1, :]) * wide).astype(BF16) for k in range(PICKS)]
    sent = dot(jnp.concatenate(choose, axis=0), jnp.concatenate(values, axis=0), ((0,), (0,)))
    back = [as_bf16(named & (place == 2 * rank + half)) for half in range(2)]
    return sent.astype(BF16), jnp.concatenate(back, axis=0)


def dispatch_kernel(routes, combine, acts, grad_out, sent_ref, back_ref, *scratch):
    held, arrived = scratch[:4], scratch[4]
    copies = [
        pltpu.make_async_copy(source, place, arrived.at[i])
        for i, (source, place) in enumerate(zip((routes, combine, acts, grad_out), held))
    ]
    for copy in copies:
        copy.start()
    for copy in copies:
        copy.wait()
    sent_ref[...], back_ref[...] = dispatch_body(*(place[...] for place in held))


def take_rows(received_ref, held):
    parts = []
    for half in range(2):
        held[half] = received_ref[:, 128 * half : 128 * (half + 1)].astype(F32)
        parts.append([held[half, pl.Slice(place, EXPERTS, 8), :] for place in range(7)])
    full = [jnp.concatenate(pair, axis=1).astype(BF16) for pair in zip(*parts)]
    return jnp.concatenate(full[:CAP], axis=0), jnp.concatenate(full[4 : 4 + CAP], axis=0)


def products(rows_x, rows_dy, w_gate, w_up, w_down):
    gate = dot(rows_x, w_gate, ((1,), (0,)))
    up = dot(rows_x, w_up, ((1,), (0,)))
    back = dot(rows_dy, w_down, ((1,), (1,)))
    cuts = [slice(half * HALF, (half + 1) * HALF) for half in range(2)]
    return [jnp.concatenate([gate[:, cut], up[:, cut], back[:, cut]], axis=1) for cut in cuts]


def split_rows(both, parity):
    even, odd = (
        jnp.concatenate([both[CHUNK * i : CHUNK * (i + 1)] for i in range(first, 8, 2)], axis=0)
        for first in range(2)
    )
    is_odd = parity == 1
    return jnp.where(is_odd, odd, even), jnp.where(is_odd, even, odd)


def product_kernel(received_ref, w_gate_ref, w_up_ref, w_down_ref, own_ref, send_ref, x_ref, dy_ref, held):
    rows_x, rows_dy = take_rows(received_ref, held)
    x_ref[...] = rows_x
    dy_ref[...] = rows_dy
    parity = jnp.bitwise_and(lax.axis_index("dp"), 1)
    for half, both in enumerate(products(rows_x, rows_dy, w_gate_ref[...], w_up_ref[...], w_down_ref[...])):
        own, other = split_rows(both, parity)
        own_ref[half] = own
        send_ref[half] = other.astype(BF16)


def first_kernel(own_ref, taken_ref, keep_ref, send_ref):
    dp = lax.axis_index("dp")
    from_partner = 1 - jnp.bitwise_and(dp, 1)
    mine = jnp.bitwise_and(lax.shift_right_logical(dp, 1), 1)
    for i in range(QUARTER):
        keep_ref[i] = own_ref[i, mine] + taken_ref[from_partner, i, mine].astype(F32)
        send_ref[i] = (own_ref[i, 1 - mine] + taken_ref[from_partner, i, 1 - mine].astype(F32)).astype(BF16)


def second_kernel(own_ref, taken_ref, out_ref, left_ref):
    dp = lax.axis_index("dp")
    from_partner = 1 - jnp.bitwise_and(lax.shift_right_logical(dp, 1), 1)
    out_ref[...] = (own_ref[...] + taken_ref[from_partner].astype(F32)).astype(BF16)
    mine = lax.shift_right_logical(dp, 2)
    kept = own_ref[mine] + taken_ref[from_partner, mine].astype(F32)
    left_ref[...] = kept - kept.astype(BF16).astype(F32)


def activate_body(parts, left):
    total = [parts[i].astype(F32) for i in range(QUARTER)]
    while len(total) > 1:
        total = [total[i] + total[i + 1] for i in range(0, len(total), 2)]
    total = total[0] + left
    pre_gate, pre_up, hidden_grad = total[:, :HALF], total[:, HALF : 2 * HALF], total[:, 2 * HALF :]
    sigmoid_gate = jax.nn.sigmoid(pre_gate)
    silu_gate = pre_gate * sigmoid_gate
    hidden = silu_gate * pre_up
    up_grad = hidden_grad * silu_gate
    gate_grad = hidden_grad * pre_up * sigmoid_gate * (1.0 + pre_gate * (1.0 - sigmoid_gate))
    return jnp.concatenate([gate_grad, up_grad, hidden], axis=1).astype(BF16)


def activate_kernel(parts_ref, left_ref, out_ref):
    out_ref[...] = activate_body(parts_ref[...], left_ref[...])


def row_grad_body(packed, w_gate, w_up):
    total = jnp.zeros((ROWS, WIDTH), F32)
    for half in range(2):
        cut = slice(half * HALF, (half + 1) * HALF)
        total += dot(packed[half][:, :HALF], w_gate[:, cut], ((1,), (1,)))
        total += dot(packed[half][:, HALF : 2 * HALF], w_up[:, cut], ((1,), (1,)))
    return total


def row_grad_kernel(packed_ref, w_gate_ref, w_up_ref, out_ref, held):
    total = row_grad_body(packed_ref[...], w_gate_ref[...], w_up_ref[...])
    for place in range(8):
        slot, half = divmod(place, 2)
        if slot < CAP:
            value = total[EXPERTS * slot : EXPERTS * (slot + 1), 128 * half : 128 * (half + 1)]
        else:
            value = jnp.zeros((EXPERTS, 128), F32)
        held[pl.Slice(place, EXPERTS, 8), :] = value
    out_ref[...] = held[...].astype(BF16)


def weight_products(packed_ref, rows_x, rows_dy, gate_ref, up_ref, down_ref):
    for half in range(2):
        cut = slice(half * HALF, (half + 1) * HALF)
        gate_ref[:, cut] = dot(rows_x, packed_ref[half, :, :HALF], ((0,), (0,))).astype(BF16)
        up_ref[:, cut] = dot(rows_x, packed_ref[half, :, HALF : 2 * HALF], ((0,), (0,))).astype(BF16)
        down_ref[cut, :] = dot(packed_ref[half, :, 2 * HALF :], rows_dy, ((0,), (0,))).astype(BF16)


def combine_body(back, returned):
    left = dot(back[:TOK], returned, ((1,), (0,)))
    right = dot(back[TOK:], returned, ((1,), (0,)))
    return jnp.concatenate([left, right], axis=1).astype(BF16)


def final_kernel(packed_ref, x_ref, dy_ref, back_ref, returned_ref, acts_ref, gate_ref, up_ref, down_ref):
    acts_ref[...] = combine_body(back_ref[...], returned_ref[...])
    weight_products(packed_ref, x_ref[...], dy_ref[...], gate_ref, up_ref, down_ref)


def call(kernel, outs, flops, *operands, **options):
    shapes = [jax.ShapeDtypeStruct(shape, dtype) for shape, dtype in outs]
    moved = sum(x.size * x.dtype.itemsize for x in [*operands, *shapes])
    return pl.pallas_call(
        kernel,
        out_shape=shapes if len(shapes) > 1 else shapes[0],
        cost_estimate=pl.CostEstimate(flops=flops, bytes_accessed=moved, transcendentals=0),
        compiler_params=pltpu.CompilerParams(vmem_limit_bytes=VMEM_LIMIT),
        **options,
    )(*operands)


HBM = pl.BlockSpec(memory_space=pltpu.HBM)
TAKEN = pltpu.VMEM((2, SLOTS, 128), F32)


def on_device(acts, grad_out, routes, combine, w_gate, w_up, w_down):
    gate_w, up_w, down_w = w_gate[0], w_up[0], w_down[0]
    matmul = 2 * ROWS * WIDTH * HIDDEN

    sent, back = call(
        dispatch_kernel,
        [((SLOTS, WIDTH), BF16), ((2 * TOK, SLOTS), BF16)],
        4 * matmul,
        *(pltpu.with_memory_space_constraint(x, pltpu.HBM) for x in (routes.T, combine.T, acts, grad_out)),
        in_specs=[HBM] * 4,
        scratch_shapes=[
            pltpu.VMEM((PICKS, TOK), jnp.int32),
            pltpu.VMEM((PICKS, TOK), F32),
            pltpu.VMEM((TOK, WIDTH), BF16),
            pltpu.VMEM((TOK, WIDTH), BF16),
            pltpu.SemaphoreType.DMA((4,)),
        ],
    )
    received = lax.all_to_all(sent.reshape(EXPERTS, 8, WIDTH), "expert", 0, 0, tiled=True)
    received = received.reshape(SLOTS, WIDTH)

    own, send, rows_x, rows_dy = call(
        product_kernel,
        [((2, ROWS // 2, PACK), F32), ((2, ROWS // 2, PACK), BF16), ((ROWS, WIDTH), BF16), ((ROWS, WIDTH), BF16)],
        3 * matmul,
        received,
        gate_w,
        up_w,
        down_w,
        scratch_shapes=[TAKEN],
    )
    mesh_axes = ("dp", "expert")
    taken = lax.all_gather(send, mesh_axes, axis=0, axis_index_groups=pairs(1))
    eighths, quarters = (QUARTER, 2, CHUNK, PACK), (QUARTER, CHUNK, PACK)
    keep, send = call(
        first_kernel,
        [(quarters, F32), (quarters, BF16)],
        ROWS * PACK,
        own.reshape(eighths),
        taken.reshape((2, *eighths)),
    )
    taken = lax.all_gather(send, mesh_axes, axis=0, axis_index_groups=pairs(2))
    parts, left = call(
        second_kernel, [(quarters, BF16), ((CHUNK, PACK), F32)], ROWS * PACK // 2, keep, taken
    )
    parts = lax.all_to_all(parts, "dp", 0, 0, tiled=True, axis_index_groups=FAR)
    block = call(activate_kernel, [((CHUNK, PACK), BF16)], 20 * CHUNK * PACK, parts, left)
    packed = lax.all_gather(block, "dp", axis=0).reshape(2, ROWS, PACK)

    row_grads = call(row_grad_kernel, [((SLOTS, 128), BF16)], 2 * matmul, packed, gate_w, up_w, scratch_shapes=[pltpu.VMEM((SLOTS, 128), F32)])
    returned = lax.all_to_all(row_grads.reshape(EXPERTS, 8, 128), "expert", 0, 0, tiled=True)
    grad_acts, new_gate, new_up, new_down = call(
        final_kernel,
        [((TOK, WIDTH), BF16), ((WIDTH, HIDDEN), BF16), ((WIDTH, HIDDEN), BF16), ((HIDDEN, WIDTH), BF16)],
        3 * matmul,
        packed,
        rows_x,
        rows_dy,
        back,
        returned.reshape(SLOTS, 128),
    )
    return grad_acts, new_gate[None], new_up[None], new_down[None]


def solution(mesh):
    return jax.shard_map(
        on_device,
        mesh=mesh,
        in_specs=(
            P("expert", "dp"),
            P("expert", "dp"),
            P("expert", None),
            P("expert", None),
            P("expert", "dp", None),
            P("expert", "dp", None),
            P("expert", None, "dp"),
        ),
        out_specs=(
            P("expert", "dp"),
            P("expert", "dp", None),
            P("expert", "dp", None),
            P("expert", None, "dp"),
        ),
        check_vma=False,
    )
```

```python
import functools

import jax
import jax.numpy as jnp
from jax import lax
from jax.experimental import pallas as pl
from jax.experimental.pallas import tpu as pltpu
from jax.sharding import PartitionSpec as P

BF16 = jnp.bfloat16
F32 = jnp.float32
TOK = 16
PICKS = 8
EXPERTS = 64
CAP = 3
ROWS = EXPERTS * CAP
WIDTH = 256
HIDDEN = 768
HALF = HIDDEN // 2
PACK = 3 * HALF
CHUNK = 24
DP = 16
SLOTS = EXPERTS * 8
QUARTER = DP // 4
FAR = [[4 * a + low for a in range(QUARTER)] for low in range(4)]


def pairs(distance):
    firsts = [dp for dp in range(DP) if not dp & distance]
    sign = [distance, -distance]
    return [
        [dp * EXPERTS + expert, (dp + sign[expert % 2]) % DP * EXPERTS + expert]
        for expert in range(EXPERTS)
        for dp in firsts
    ]


VMEM_LIMIT = 24 * 1024 * 1024


def dot(a, b, contract):
    return lax.dot_general(a, b, (contract, ((), ())), preferred_element_type=F32)


def iota(shape, dim):
    return lax.broadcasted_iota(jnp.int32, shape, dim)


def column(row):
    diagonal = iota((TOK, TOK), 0) == iota((TOK, TOK), 1)
    spread = jnp.where(diagonal, jnp.broadcast_to(row, (TOK, TOK)), jnp.zeros((), row.dtype))
    return jnp.sum(spread, axis=1, keepdims=True)


def slots_of(routes_t):
    expert = lax.shift_right_logical(iota((TOK, SLOTS), 1), 3)
    hits = [column(routes_t[k : k + 1, :]) == expert for k in range(PICKS)]
    named = functools.reduce(jnp.logical_or, hits)
    counts = named.astype(F32)
    row = iota((TOK, SLOTS), 0)
    running = counts
    for step in (1, 2, 4, 8):
        running += jnp.where(row >= step, jnp.roll(running, step, axis=0), 0.0)
    rank = (running - counts).astype(jnp.int32)
    return hits, named, rank


def as_bf16(mask):
    return mask.astype(F32).astype(BF16)


def dispatch_body(routes_t, combine_t, acts, grad_out):
    hits, named, rank = slots_of(routes_t)
    place = jnp.bitwise_and(iota((TOK, SLOTS), 1), 7)
    wanted_x = place == rank
    wanted_dy = place == rank + 4
    choose = [as_bf16(named & wanted_x)] + [as_bf16(hit & wanted_dy) for hit in hits]
    wide = grad_out.astype(F32)
    values = [acts] + [(column(combine_t[k : k + 1, :]) * wide).astype(BF16) for k in range(PICKS)]
    sent = dot(jnp.concatenate(choose, axis=0), jnp.concatenate(values, axis=0), ((0,), (0,)))
    back = [as_bf16(named & (place == 2 * rank + half)) for half in range(2)]
    return sent.astype(BF16), jnp.concatenate(back, axis=0)


def dispatch_kernel(routes, combine, acts, grad_out, sent_ref, back_ref, *scratch):
    held, arrived = scratch[:4], scratch[4]
    copies = [
        pltpu.make_async_copy(source, place, arrived.at[i])
        for i, (source, place) in enumerate(zip((routes, combine, acts, grad_out), held))
    ]
    for copy in copies:
        copy.start()
    for copy in copies:
        copy.wait()
    sent_ref[...], back_ref[...] = dispatch_body(*(place[...] for place in held))


def take_rows(received_ref, held):
    parts = []
    for half in range(2):
        held[half] = received_ref[:, 128 * half : 128 * (half + 1)].astype(F32)
        parts.append([held[half, pl.Slice(place, EXPERTS, 8), :] for place in range(7)])
    full = [jnp.concatenate(pair, axis=1).astype(BF16) for pair in zip(*parts)]
    return jnp.concatenate(full[:CAP], axis=0), jnp.concatenate(full[4 : 4 + CAP], axis=0)


def products(rows_x, rows_dy, w_gate, w_up, w_down):
    gate = dot(rows_x, w_gate, ((1,), (0,)))
    up = dot(rows_x, w_up, ((1,), (0,)))
    back = dot(rows_dy, w_down, ((1,), (1,)))
    cuts = [slice(half * HALF, (half + 1) * HALF) for half in range(2)]
    return [jnp.concatenate([gate[:, cut], up[:, cut], back[:, cut]], axis=1) for cut in cuts]


def split_rows(both, parity):
    even, odd = (
        jnp.concatenate([both[CHUNK * i : CHUNK * (i + 1)] for i in range(first, 8, 2)], axis=0)
        for first in range(2)
    )
    is_odd = parity == 1
    return jnp.where(is_odd, odd, even), jnp.where(is_odd, even, odd)


def product_kernel(received_ref, w_gate_ref, w_up_ref, w_down_ref, own_ref, send_ref, x_ref, dy_ref, held):
    rows_x, rows_dy = take_rows(received_ref, held)
    x_ref[...] = reorder(rows_x.astype(F32)).astype(BF16)
    dy_ref[...] = reorder(rows_dy.astype(F32)).astype(BF16)
    parity = jnp.bitwise_and(lax.axis_index("dp"), 1)
    for half, both in enumerate(products(rows_x, rows_dy, w_gate_ref[...], w_up_ref[...], w_down_ref[...])):
        own, other = split_rows(both, parity)
        own_ref[half] = own
        send_ref[half] = other.astype(BF16)


def first_kernel(own_ref, taken_ref, keep_ref, send_ref):
    dp = lax.axis_index("dp")
    from_partner = 1 - jnp.bitwise_and(dp, 1)
    mine = jnp.bitwise_and(lax.shift_right_logical(dp, 1), 1)
    for i in range(QUARTER):
        keep_ref[i] = own_ref[i, mine] + taken_ref[from_partner, i, mine].astype(F32)
        send_ref[i] = (own_ref[i, 1 - mine] + taken_ref[from_partner, i, 1 - mine].astype(F32)).astype(BF16)


def second_kernel(own_ref, taken_ref, out_ref, sum_ref):
    from_partner = 1 - jnp.bitwise_and(lax.shift_right_logical(lax.axis_index("dp"), 1), 1)
    total = own_ref[...] + taken_ref[from_partner].astype(F32)
    sum_ref[...] = total
    out_ref[...] = total.astype(BF16)


def activate_body(parts, own):
    wide = [part.astype(F32) for part in parts]
    total = (wide[0] + wide[1]) + (wide[2] + wide[3]) + (own - own.astype(BF16).astype(F32))
    pre_gate, pre_up, hidden_grad = total[:, :HALF], total[:, HALF : 2 * HALF], total[:, 2 * HALF :]
    sigmoid_gate = jax.nn.sigmoid(pre_gate)
    silu_gate = pre_gate * sigmoid_gate
    hidden = silu_gate * pre_up
    up_grad = hidden_grad * silu_gate
    gate_grad = hidden_grad * pre_up * sigmoid_gate * (1.0 + pre_gate * (1.0 - sigmoid_gate))
    return jnp.concatenate([gate_grad, up_grad, hidden], axis=1).astype(BF16)


def activate_kernel(parts_ref, sum_ref, out_ref):
    for i in range(QUARTER):
        out_ref[i] = activate_body([parts_ref[k, i] for k in range(QUARTER)], sum_ref[i])


def reorder(rows):
    return jnp.concatenate([rows[CHUNK * i : CHUNK * (i + 1)] for i in (0, 4, 2, 6, 1, 5, 3, 7)], axis=0)


def half_of(packed_ref, half, first, last):
    return jnp.concatenate([packed_ref[i, half, :, first:last] for i in range(4)], axis=0)


def row_grad_body(packed_ref, w_gate, w_up):
    total = jnp.zeros((ROWS, WIDTH), F32)
    for half in range(2):
        cut = slice(half * HALF, (half + 1) * HALF)
        total += dot(half_of(packed_ref, half, 0, HALF), w_gate[:, cut], ((1,), (1,)))
        total += dot(half_of(packed_ref, half, HALF, 2 * HALF), w_up[:, cut], ((1,), (1,)))
    return reorder(total)


def row_grad_kernel(packed_ref, w_gate_ref, w_up_ref, out_ref, held):
    total = row_grad_body(packed_ref, w_gate_ref[...], w_up_ref[...])
    for place in range(8):
        slot, half = divmod(place, 2)
        if slot < CAP:
            value = total[EXPERTS * slot : EXPERTS * (slot + 1), 128 * half : 128 * (half + 1)]
        else:
            value = jnp.zeros((EXPERTS, 128), F32)
        held[pl.Slice(place, EXPERTS, 8), :] = value
    out_ref[...] = held[...].astype(BF16)


def weight_products(packed_ref, rows_x, rows_dy, gate_ref, up_ref, down_ref):
    for half in range(2):
        cut = slice(half * HALF, (half + 1) * HALF)
        gate_ref[:, cut] = dot(rows_x, half_of(packed_ref, half, 0, HALF), ((0,), (0,))).astype(BF16)
        up_ref[:, cut] = dot(rows_x, half_of(packed_ref, half, HALF, 2 * HALF), ((0,), (0,))).astype(BF16)
        down_ref[cut, :] = dot(half_of(packed_ref, half, 2 * HALF, PACK), rows_dy, ((0,), (0,))).astype(BF16)


def combine_body(back, returned):
    left = dot(back[:TOK], returned, ((1,), (0,)))
    right = dot(back[TOK:], returned, ((1,), (0,)))
    return jnp.concatenate([left, right], axis=1).astype(BF16)


def final_kernel(packed_ref, x_ref, dy_ref, back_ref, returned_ref, acts_ref, gate_ref, up_ref, down_ref):
    acts_ref[...] = combine_body(back_ref[...], returned_ref[...])
    weight_products(packed_ref, x_ref[...], dy_ref[...], gate_ref, up_ref, down_ref)


def call(kernel, outs, flops, *operands, **options):
    shapes = [jax.ShapeDtypeStruct(shape, dtype) for shape, dtype in outs]
    moved = sum(x.size * x.dtype.itemsize for x in [*operands, *shapes])
    return pl.pallas_call(
        kernel,
        out_shape=shapes if len(shapes) > 1 else shapes[0],
        cost_estimate=pl.CostEstimate(flops=flops, bytes_accessed=moved, transcendentals=0),
        compiler_params=pltpu.CompilerParams(vmem_limit_bytes=VMEM_LIMIT),
        **options,
    )(*operands)


HBM = pl.BlockSpec(memory_space=pltpu.HBM)
TAKEN = pltpu.VMEM((2, SLOTS, 128), F32)


def on_device(acts, grad_out, routes, combine, w_gate, w_up, w_down):
    gate_w, up_w, down_w = w_gate[0], w_up[0], w_down[0]
    matmul = 2 * ROWS * WIDTH * HIDDEN

    sent, back = call(
        dispatch_kernel,
        [((SLOTS, WIDTH), BF16), ((2 * TOK, SLOTS), BF16)],
        4 * matmul,
        *(pltpu.with_memory_space_constraint(x, pltpu.HBM) for x in (routes.T, combine.T, acts, grad_out)),
        in_specs=[HBM] * 4,
        scratch_shapes=[
            pltpu.VMEM((PICKS, TOK), jnp.int32),
            pltpu.VMEM((PICKS, TOK), F32),
            pltpu.VMEM((TOK, WIDTH), BF16),
            pltpu.VMEM((TOK, WIDTH), BF16),
            pltpu.SemaphoreType.DMA((4,)),
        ],
    )
    received = lax.all_to_all(sent.reshape(EXPERTS, 8, WIDTH), "expert", 0, 0, tiled=True)
    received = received.reshape(SLOTS, WIDTH)

    own, send, rows_x, rows_dy = call(
        product_kernel,
        [((2, ROWS // 2, PACK), F32), ((2, ROWS // 2, PACK), BF16), ((ROWS, WIDTH), BF16), ((ROWS, WIDTH), BF16)],
        3 * matmul,
        received,
        gate_w,
        up_w,
        down_w,
        scratch_shapes=[TAKEN],
    )
    mesh_axes = ("dp", "expert")
    taken = lax.all_gather(send, mesh_axes, axis=0, axis_index_groups=pairs(1))
    eighths, quarters = (QUARTER, 2, CHUNK, PACK), (QUARTER, CHUNK, PACK)
    keep, send = call(
        first_kernel,
        [(quarters, F32), (quarters, BF16)],
        ROWS * PACK,
        own.reshape(eighths),
        taken.reshape((2, *eighths)),
    )
    taken = lax.all_gather(send, mesh_axes, axis=0, axis_index_groups=pairs(2))
    parts, total = call(second_kernel, [(quarters, BF16), (quarters, F32)], ROWS * PACK // 2, keep, taken)
    parts = lax.all_gather(parts, "dp", axis=0, axis_index_groups=FAR)
    block = call(activate_kernel, [(quarters, BF16)], 80 * CHUNK * PACK, parts, total)
    block = lax.all_gather(block, mesh_axes, axis=0, axis_index_groups=pairs(2))
    packed = lax.all_gather(block, mesh_axes, axis=0, axis_index_groups=pairs(1)).reshape(4, 2, 2 * CHUNK, PACK)

    row_grads = call(row_grad_kernel, [((SLOTS, 128), BF16)], 2 * matmul, packed, gate_w, up_w, scratch_shapes=[pltpu.VMEM((SLOTS, 128), F32)])
    returned = lax.all_to_all(row_grads.reshape(EXPERTS, 8, 128), "expert", 0, 0, tiled=True)
    grad_acts, new_gate, new_up, new_down = call(
        final_kernel,
        [((TOK, WIDTH), BF16), ((WIDTH, HIDDEN), BF16), ((WIDTH, HIDDEN), BF16), ((HIDDEN, WIDTH), BF16)],
        3 * matmul,
        packed,
        rows_x,
        rows_dy,
        back,
        returned.reshape(SLOTS, 128),
    )
    return grad_acts, new_gate[None], new_up[None], new_down[None]


def solution(mesh):
    return jax.shard_map(
        on_device,
        mesh=mesh,
        in_specs=(
            P("expert", "dp"),
            P("expert", "dp"),
            P("expert", None),
            P("expert", None),
            P("expert", "dp", None),
            P("expert", "dp", None),
            P("expert", None, "dp"),
        ),
        out_specs=(
            P("expert", "dp"),
            P("expert", "dp", None),
            P("expert", "dp", None),
            P("expert", None, "dp"),
        ),
        check_vma=False,
    )
```

```python
import functools

import jax
import jax.numpy as jnp
from jax import lax
from jax.experimental import pallas as pl
from jax.experimental.pallas import tpu as pltpu
from jax.sharding import PartitionSpec as P

BF16 = jnp.bfloat16
F32 = jnp.float32
TOK = 16
PICKS = 8
EXPERTS = 64
CAP = 3
ROWS = EXPERTS * CAP
WIDTH = 256
HIDDEN = 768
HALF = HIDDEN // 2
PACK = 3 * HALF
CHUNK = 24
DP = 16
SLOTS = EXPERTS * 8
QUARTER = DP // 4
FAR = [[4 * a + low for a in range(QUARTER)] for low in range(4)]


NEAR = [
    [(4 * first + 2 * (expert % 2) + i) % DP * EXPERTS + expert for i in range(4)]
    for expert in range(EXPERTS)
    for first in range(QUARTER)
]


def pairs(distance):
    firsts = [dp for dp in range(DP) if not dp & distance]
    sign = [distance, -distance]
    return [
        [dp * EXPERTS + expert, (dp + sign[expert % 2]) % DP * EXPERTS + expert]
        for expert in range(EXPERTS)
        for dp in firsts
    ]


VMEM_LIMIT = 24 * 1024 * 1024


def dot(a, b, contract):
    return lax.dot_general(a, b, (contract, ((), ())), preferred_element_type=F32)


def iota(shape, dim):
    return lax.broadcasted_iota(jnp.int32, shape, dim)


def column(row):
    diagonal = iota((TOK, TOK), 0) == iota((TOK, TOK), 1)
    spread = jnp.where(diagonal, jnp.broadcast_to(row, (TOK, TOK)), jnp.zeros((), row.dtype))
    return jnp.sum(spread, axis=1, keepdims=True)


def slots_of(routes_t):
    expert = lax.shift_right_logical(iota((TOK, SLOTS), 1), 3)
    hits = [column(routes_t[k : k + 1, :]) == expert for k in range(PICKS)]
    named = functools.reduce(jnp.logical_or, hits)
    counts = named.astype(F32)
    row = iota((TOK, SLOTS), 0)
    running = counts
    for step in (1, 2, 4, 8):
        running += jnp.where(row >= step, jnp.roll(running, step, axis=0), 0.0)
    rank = (running - counts).astype(jnp.int32)
    return hits, named, rank


def as_bf16(mask):
    return mask.astype(F32).astype(BF16)


def dispatch_body(routes_t, combine_t, acts, grad_out):
    hits, named, rank = slots_of(routes_t)
    place = jnp.bitwise_and(iota((TOK, SLOTS), 1), 7)
    wanted_x = place == rank
    wanted_dy = place == rank + 4
    choose = [as_bf16(named & wanted_x)] + [as_bf16(hit & wanted_dy) for hit in hits]
    wide = grad_out.astype(F32)
    values = [acts] + [(column(combine_t[k : k + 1, :]) * wide).astype(BF16) for k in range(PICKS)]
    sent = dot(jnp.concatenate(choose, axis=0), jnp.concatenate(values, axis=0), ((0,), (0,)))
    back = [as_bf16(named & (place == 2 * rank + half)) for half in range(2)]
    return sent.astype(BF16), jnp.concatenate(back, axis=0)


def dispatch_kernel(routes, combine, acts, grad_out, sent_ref, back_ref, *scratch):
    held, arrived = scratch[:4], scratch[4]
    copies = [
        pltpu.make_async_copy(source, place, arrived.at[i])
        for i, (source, place) in enumerate(zip((routes, combine, acts, grad_out), held))
    ]
    for copy in copies:
        copy.start()
    for copy in copies:
        copy.wait()
    sent_ref[...], back_ref[...] = dispatch_body(*(place[...] for place in held))


def take_rows(received_ref, held):
    parts = []
    for half in range(2):
        held[half] = received_ref[:, 128 * half : 128 * (half + 1)].astype(F32)
        parts.append([held[half, pl.Slice(place, EXPERTS, 8), :] for place in range(7)])
    full = [jnp.concatenate(pair, axis=1).astype(BF16) for pair in zip(*parts)]
    return jnp.concatenate(full[:CAP], axis=0), jnp.concatenate(full[4 : 4 + CAP], axis=0)


def products(rows_x, rows_dy, w_gate, w_up, w_down):
    gate = dot(rows_x, w_gate, ((1,), (0,)))
    up = dot(rows_x, w_up, ((1,), (0,)))
    back = dot(rows_dy, w_down, ((1,), (1,)))
    cuts = [slice(half * HALF, (half + 1) * HALF) for half in range(2)]
    return [jnp.concatenate([gate[:, cut], up[:, cut], back[:, cut]], axis=1) for cut in cuts]


def split_rows(both, parity):
    even, odd = (
        jnp.concatenate([both[CHUNK * i : CHUNK * (i + 1)] for i in range(first, 8, 2)], axis=0)
        for first in range(2)
    )
    is_odd = parity == 1
    return jnp.where(is_odd, odd, even), jnp.where(is_odd, even, odd)


def product_kernel(received_ref, w_gate_ref, w_up_ref, w_down_ref, own_ref, send_ref, x_ref, dy_ref, held):
    rows_x, rows_dy = take_rows(received_ref, held)
    x_ref[...] = reorder(rows_x.astype(F32)).astype(BF16)
    dy_ref[...] = reorder(rows_dy.astype(F32)).astype(BF16)
    parity = jnp.bitwise_and(lax.axis_index("dp"), 1)
    for half, both in enumerate(products(rows_x, rows_dy, w_gate_ref[...], w_up_ref[...], w_down_ref[...])):
        own, other = split_rows(both, parity)
        own_ref[half] = own
        send_ref[half] = other.astype(BF16)


def first_kernel(own_ref, taken_ref, keep_ref, send_ref):
    dp = lax.axis_index("dp")
    from_partner = 1 - jnp.bitwise_and(dp, 1)
    mine = jnp.bitwise_and(lax.shift_right_logical(dp, 1), 1)
    for i in range(QUARTER):
        keep_ref[i] = own_ref[i, mine] + taken_ref[from_partner, i, mine].astype(F32)
        send_ref[i] = (own_ref[i, 1 - mine] + taken_ref[from_partner, i, 1 - mine].astype(F32)).astype(BF16)


def second_kernel(own_ref, taken_ref, out_ref, sum_ref):
    from_partner = 1 - jnp.bitwise_and(lax.shift_right_logical(lax.axis_index("dp"), 1), 1)
    total = own_ref[...] + taken_ref[from_partner].astype(F32)
    sum_ref[...] = total
    out_ref[...] = total.astype(BF16)


def activate_body(parts, own):
    wide = [part.astype(F32) for part in parts]
    total = (wide[0] + wide[1]) + (wide[2] + wide[3]) + (own - own.astype(BF16).astype(F32))
    pre_gate, pre_up, hidden_grad = total[:, :HALF], total[:, HALF : 2 * HALF], total[:, 2 * HALF :]
    sigmoid_gate = jax.nn.sigmoid(pre_gate)
    silu_gate = pre_gate * sigmoid_gate
    hidden = silu_gate * pre_up
    up_grad = hidden_grad * silu_gate
    gate_grad = hidden_grad * pre_up * sigmoid_gate * (1.0 + pre_gate * (1.0 - sigmoid_gate))
    return jnp.concatenate([gate_grad, up_grad, hidden], axis=1).astype(BF16)


def activate_kernel(parts_ref, sum_ref, out_ref):
    for i in range(QUARTER):
        out_ref[i] = activate_body([parts_ref[k, i] for k in range(QUARTER)], sum_ref[i])


def reorder(rows):
    return jnp.concatenate([rows[CHUNK * i : CHUNK * (i + 1)] for i in (0, 4, 2, 6, 1, 5, 3, 7)], axis=0)


def half_of(packed_ref, half, first, last):
    flip = 2 * jnp.bitwise_and(lax.axis_index("expert"), 1)
    places = [jnp.bitwise_xor(flip, low) for low in (0, 2, 1, 3)]
    return jnp.concatenate([packed_ref[place, half, :, first:last] for place in places], axis=0)


def row_grad_body(packed_ref, w_gate, w_up):
    total = jnp.zeros((ROWS, WIDTH), F32)
    for half in range(2):
        cut = slice(half * HALF, (half + 1) * HALF)
        total += dot(half_of(packed_ref, half, 0, HALF), w_gate[:, cut], ((1,), (1,)))
        total += dot(half_of(packed_ref, half, HALF, 2 * HALF), w_up[:, cut], ((1,), (1,)))
    return reorder(total)


def row_grad_kernel(packed_ref, w_gate_ref, w_up_ref, out_ref, held):
    total = row_grad_body(packed_ref, w_gate_ref[...], w_up_ref[...])
    for place in range(8):
        slot, half = divmod(place, 2)
        if slot < CAP:
            value = total[EXPERTS * slot : EXPERTS * (slot + 1), 128 * half : 128 * (half + 1)]
        else:
            value = jnp.zeros((EXPERTS, 128), F32)
        held[pl.Slice(place, EXPERTS, 8), :] = value
    out_ref[...] = held[...].astype(BF16)


def weight_products(packed_ref, rows_x, rows_dy, gate_ref, up_ref, down_ref):
    for half in range(2):
        cut = slice(half * HALF, (half + 1) * HALF)
        gate_ref[:, cut] = dot(rows_x, half_of(packed_ref, half, 0, HALF), ((0,), (0,))).astype(BF16)
        up_ref[:, cut] = dot(rows_x, half_of(packed_ref, half, HALF, 2 * HALF), ((0,), (0,))).astype(BF16)
        down_ref[cut, :] = dot(half_of(packed_ref, half, 2 * HALF, PACK), rows_dy, ((0,), (0,))).astype(BF16)


def combine_body(back, returned):
    left = dot(back[:TOK], returned, ((1,), (0,)))
    right = dot(back[TOK:], returned, ((1,), (0,)))
    return jnp.concatenate([left, right], axis=1).astype(BF16)


def final_kernel(packed_ref, x_ref, dy_ref, back_ref, returned_ref, acts_ref, gate_ref, up_ref, down_ref):
    acts_ref[...] = combine_body(back_ref[...], returned_ref[...])
    weight_products(packed_ref, x_ref[...], dy_ref[...], gate_ref, up_ref, down_ref)


def call(kernel, outs, flops, *operands, **options):
    shapes = [jax.ShapeDtypeStruct(shape, dtype) for shape, dtype in outs]
    moved = sum(x.size * x.dtype.itemsize for x in [*operands, *shapes])
    return pl.pallas_call(
        kernel,
        out_shape=shapes if len(shapes) > 1 else shapes[0],
        cost_estimate=pl.CostEstimate(flops=flops, bytes_accessed=moved, transcendentals=0),
        compiler_params=pltpu.CompilerParams(vmem_limit_bytes=VMEM_LIMIT),
        **options,
    )(*operands)


HBM = pl.BlockSpec(memory_space=pltpu.HBM)
TAKEN = pltpu.VMEM((2, SLOTS, 128), F32)


def on_device(acts, grad_out, routes, combine, w_gate, w_up, w_down):
    gate_w, up_w, down_w = w_gate[0], w_up[0], w_down[0]
    matmul = 2 * ROWS * WIDTH * HIDDEN

    sent, back = call(
        dispatch_kernel,
        [((SLOTS, WIDTH), BF16), ((2 * TOK, SLOTS), BF16)],
        4 * matmul,
        *(pltpu.with_memory_space_constraint(x, pltpu.HBM) for x in (routes.T, combine.T, acts, grad_out)),
        in_specs=[HBM] * 4,
        scratch_shapes=[
            pltpu.VMEM((PICKS, TOK), jnp.int32),
            pltpu.VMEM((PICKS, TOK), F32),
            pltpu.VMEM((TOK, WIDTH), BF16),
            pltpu.VMEM((TOK, WIDTH), BF16),
            pltpu.SemaphoreType.DMA((4,)),
        ],
    )
    received = lax.all_to_all(sent.reshape(EXPERTS, 8, WIDTH), "expert", 0, 0, tiled=True)
    received = received.reshape(SLOTS, WIDTH)

    own, send, rows_x, rows_dy = call(
        product_kernel,
        [((2, ROWS // 2, PACK), F32), ((2, ROWS // 2, PACK), BF16), ((ROWS, WIDTH), BF16), ((ROWS, WIDTH), BF16)],
        3 * matmul,
        received,
        gate_w,
        up_w,
        down_w,
        scratch_shapes=[TAKEN],
    )
    mesh_axes = ("dp", "expert")
    taken = lax.all_gather(send, mesh_axes, axis=0, axis_index_groups=pairs(1))
    eighths, quarters = (QUARTER, 2, CHUNK, PACK), (QUARTER, CHUNK, PACK)
    keep, send = call(
        first_kernel,
        [(quarters, F32), (quarters, BF16)],
        ROWS * PACK,
        own.reshape(eighths),
        taken.reshape((2, *eighths)),
    )
    taken = lax.all_gather(send, mesh_axes, axis=0, axis_index_groups=pairs(2))
    parts, total = call(second_kernel, [(quarters, BF16), (quarters, F32)], ROWS * PACK // 2, keep, taken)
    parts = lax.all_gather(parts, "dp", axis=0, axis_index_groups=FAR)
    block = call(activate_kernel, [(quarters, BF16)], 80 * CHUNK * PACK, parts, total)
    packed = lax.all_gather(block, mesh_axes, axis=0, axis_index_groups=NEAR).reshape(4, 2, 2 * CHUNK, PACK)

    row_grads = call(row_grad_kernel, [((SLOTS, 128), BF16)], 2 * matmul, packed, gate_w, up_w, scratch_shapes=[pltpu.VMEM((SLOTS, 128), F32)])
    returned = lax.all_to_all(row_grads.reshape(EXPERTS, 8, 128), "expert", 0, 0, tiled=True)
    grad_acts, new_gate, new_up, new_down = call(
        final_kernel,
        [((TOK, WIDTH), BF16), ((WIDTH, HIDDEN), BF16), ((WIDTH, HIDDEN), BF16), ((HIDDEN, WIDTH), BF16)],
        3 * matmul,
        packed,
        rows_x,
        rows_dy,
        back,
        returned.reshape(SLOTS, 128),
    )
    return grad_acts, new_gate[None], new_up[None], new_down[None]


def solution(mesh):
    return jax.shard_map(
        on_device,
        mesh=mesh,
        in_specs=(
            P("expert", "dp"),
            P("expert", "dp"),
            P("expert", None),
            P("expert", None),
            P("expert", "dp", None),
            P("expert", "dp", None),
            P("expert", None, "dp"),
        ),
        out_specs=(
            P("expert", "dp"),
            P("expert", "dp", None),
            P("expert", "dp", None),
            P("expert", None, "dp"),
        ),
        check_vma=False,
    )
```
